32 devices in a mesh: row: 4 (over y, core), col: 8 (over z, x).
Axes of the slice: x: 2, y: 2, z: 4, core: 2. Of those that a mesh axis runs over, the one named last changes fastest.
Arguments:
- seq_ids: int32 [1024], replicated, may hold values from 0 to 3, never falling along the last dimension, each value on 1 to 512 neighbouring positions
- query_inputs: bfloat16 [1024, 8192], P('col', 'row'), may hold values from -6 to 6
- query_grads: bfloat16 [1024, 8192], P('row', 'col'), may hold values from -0.25 to 0.25
- query_act_basis: bfloat16 [8192, 8192], P('row', 'col'), may hold values from -0.0625 to 0.0625
- query_grad_basis: bfloat16 [8192, 8192], P('col', 'row'), may hold values from -0.0625 to 0.0625
- output_inputs: bfloat16 [1024, 8192], P('col', 'row'), may hold values from -6 to 6
- output_grads: bfloat16 [1024, 8192], P('row', 'col'), may hold values from -0.25 to 0.25
- output_act_basis: bfloat16 [8192, 8192], P('row', 'col'), may hold values from -0.0625 to 0.0625
- output_grad_basis: bfloat16 [8192, 8192], P('col', 'row'), may hold values from -0.0625 to 0.0625
Outputs:
- query_corr: float32 [8192, 8192], P('row', 'col')
- output_corr: float32 [8192, 8192], P('row', 'col')
The draws below stay inside these ranges and needn't reach their ends.
Inputs may be any that keep to these rules, and one draw needn't show every extreme that they name: seq_ids never falls along the tokens; each of the 4 sequences holds 1 to 512 tokens, and one holds exactly 512.
All inputs are finite; a program needn't handle non-finite values.
Results may differ from the reference program's by a relative error of at most 0.0003.
Values may be sent and summed in bfloat16 or wider, within the bound.
A program may use at most 128 MiB of HBM per device.

```python
import math
import jax
import jax.numpy as jnp
import numpy as np
from jax import lax

D = 8192
TOKENS = 1024
SEQS = 4
MOST = 512


def block_levels(key, extent, cuts, low, largest):
    factor_of, own = 1.0, jax.random.fold_in(key, 6)
    for position, parts in cuts:
        steps = jnp.exp(jax.random.uniform(jax.random.fold_in(own, position), (parts,), jnp.float32, low / len(cuts), largest / len(cuts)))
        factor_of = factor_of * jnp.repeat(steps, extent[position] // parts).reshape([-1 if axis == position else 1 for axis in range(len(extent))])
    return factor_of


def profile(count, total, bound, lean):
    portions = [(1 << 20) // math.isqrt(standing ** lean) + 1 for standing in range(2, count + 1)]
    spare, given = total - bound - (count - 1), [1] * (count - 1)
    while spare > 0:
        free = [i for i in range(count - 1) if given[i] < bound]
        pool, budget = sum([portions[i] for i in free]), spare
        for i in free:
            more = min(bound - given[i], max(1, budget * portions[i] // pool), spare)
            given[i] = given[i] + more
            spare = spare - more
    return np.array([bound] + given)


def ragged_sizes(stream_key, count, total, reach, skew):
    if count == 2:
        one = jax.random.randint(stream_key, (), max(1, total - reach), min(reach, total - 1) + 1)
        return jnp.stack([one, total - one])
    sizes = jnp.asarray(profile(count, total, reach, skew), jnp.int32)
    couples = (count - 1) // 2
    source_of, taker = sizes[1:1 + 2 * couples:2], sizes[2:2 + 2 * couples:2]
    margin = jnp.minimum(source_of - 1, reach - taker)
    moved = jax.random.randint(jax.random.fold_in(stream_key, 1), (couples,), 0, 1 << 20) % (margin + 1)
    sizes = sizes.at[1:1 + 2 * couples:2].set(source_of - moved).at[2:2 + 2 * couples:2].set(taker + moved)
    return sizes[jax.random.permutation(jax.random.fold_in(stream_key, 2), count)]


def bell_draw(rng, shape, width, reach, cuts=(), kind=jnp.bfloat16):
    level = block_levels(rng, shape, cuts, -0.22, 0.18) if cuts else 1.0
    values = jax.random.normal(rng, shape, jnp.float32) * width * level
    return jnp.minimum(jnp.maximum(values, -reach), reach).astype(kind)


def setup_inputs(seed: int = 0) -> dict:
    key_list = jax.random.split(jax.random.key(seed), 10)
    return {
        "seq_ids": jnp.searchsorted(jnp.cumsum(ragged_sizes(key_list[0], SEQS, TOKENS, MOST, 2)), jnp.arange(TOKENS), side="right").astype(jnp.int32),
        "query_inputs": bell_draw(key_list[1], (TOKENS, D), 1.0, 6.0, ((0, 8), (1, 4))),
        "query_grads": bell_draw(key_list[2], (TOKENS, D), MOST ** -0.5, 0.25, ((0, 4), (1, 8))),
        "query_act_basis": bell_draw(key_list[3], (D, D), D ** -0.5, 0.0625, ((0, 4), (1, 8))),
        "query_grad_basis": bell_draw(key_list[4], (D, D), D ** -0.5, 0.0625, ((0, 8), (1, 4))),
        "output_inputs": bell_draw(key_list[5], (TOKENS, D), 1.0, 6.0, ((0, 8), (1, 4))),
        "output_grads": bell_draw(key_list[6], (TOKENS, D), MOST ** -0.5, 0.25, ((0, 4), (1, 8))),
        "output_act_basis": bell_draw(key_list[7], (D, D), D ** -0.5, 0.0625, ((0, 4), (1, 8))),
        "output_grad_basis": bell_draw(key_list[8], (D, D), D ** -0.5, 0.0625, ((0, 8), (1, 4))),
    }


def rotate(tokens, eigen_basis):
    return jnp.dot(tokens, eigen_basis, preferred_element_type=jnp.float32)


def correct(act_rot, grad_rot, seq_ids):
    numbers = jnp.arange(SEQS, dtype=jnp.int32)
    counts = jnp.sum((seq_ids[None, :] == numbers[:, None]).astype(jnp.int32), axis=1).astype(jnp.int32)
    starts = (jnp.cumsum(counts) - counts).astype(jnp.int32)
    padded_act = jnp.concatenate([act_rot, jnp.zeros((MOST, act_rot.shape[1]), act_rot.dtype)], 0)
    padded_grad = jnp.concatenate([grad_rot, jnp.zeros((MOST, grad_rot.shape[1]), grad_rot.dtype)], 0)
    offsets = jnp.arange(MOST, dtype=jnp.int32)
    running = jnp.zeros((grad_rot.shape[1], act_rot.shape[1]), jnp.float32)
    for seq_index in range(SEQS):
        act_rows = lax.dynamic_slice_in_dim(padded_act, starts[seq_index], MOST, 0)
        grad_rows = lax.dynamic_slice_in_dim(padded_grad, starts[seq_index], MOST, 0)
        inside = offsets < counts[seq_index]
        grad_rows = jnp.where(inside[:, None], grad_rows, jnp.zeros_like(grad_rows))
        product = lax.dot_general(grad_rows, act_rows, (((0,), (0,)), ((), ())), precision=lax.Precision.HIGHEST)
        running = running + product * product
    return running / SEQS


def reference(seq_ids, query_inputs, query_grads, query_act_basis, query_grad_basis, output_inputs, output_grads, output_act_basis, output_grad_basis):
    query_corr = correct(rotate(query_inputs, query_act_basis), rotate(query_grads, query_grad_basis), seq_ids)
    output_corr = correct(rotate(output_inputs, output_act_basis), rotate(output_grads, output_grad_basis), seq_ids)
    return (query_corr, output_corr)
```

```python
import functools

import jax
import jax.numpy as jnp
from jax import lax
from jax.experimental import pallas as pl
from jax.experimental.pallas import tpu as pltpu
from jax.sharding import PartitionSpec as P

SEQS = 4
CHUNK = 16
TOP = 32767.0
MESH = pl.DeviceIdType.MESH
F32, BF16, I16, I32 = jnp.float32, jnp.bfloat16, jnp.int16, jnp.int32


def quantize(load, store, store_scale, chunks, width):
    most = lax.fori_loop(
        0, chunks, lambda i, m: jnp.maximum(m, jnp.abs(load(i))), jnp.zeros((CHUNK, width), F32)
    )
    most = jnp.max(jnp.max(most, axis=1, keepdims=True), axis=0, keepdims=True)
    inverse = jnp.where(most > 1e-30, TOP / jnp.maximum(most, 1e-30), 0.0)
    store_scale(jnp.broadcast_to(most * (1.0 / TOP), (8, 128)))

    def body(i, carry):
        store(i, jnp.round(load(i) * inverse).astype(I32).astype(I16))
        return carry

    lax.fori_loop(0, chunks, body, 0)


def widen(codes, scale):
    return codes.astype(I32).astype(F32) * scale


def rows_of(i, size):
    return pl.ds(pl.multiple_of(i * size, size), size)


def rotate_kernel(n_row, n_col, *refs):
    ins, refs = (refs[0:4], refs[4:8]), refs[8:]
    outs, refs = (refs[0:4], refs[4:8]), refs[8:]
    (grads_all, inputs_all, basis_g, basis_a, block, own, xsend, xsend_s, xrecv, xrecv_s, zrecv, zrecv_s,
     fin, fin_s, aown, asend, asend_s, arecv, arecv_s, afin, afin_s,
     g_send, g_recv, i_send, f_send, i_recv, xs_send, xs_recv, zs_send, zs_recv,
     ag_send, agf_send, ag_recv, as_send, as_recv, aa_send, aa_recv, local) = refs

    r, c = lax.axis_index("row"), lax.axis_index("col")
    nz = n_col // 2
    z, x = c // 2, lax.rem(c, 2)
    partner = (r, z * 2 + 1 - x)
    tokens, feats_g = grads_all.shape[1:]
    feats_a = inputs_all.shape[2]
    width_g, width_a = basis_g.shape[2], basis_a.shape[2]
    t_col, t_row = tokens // n_col, tokens // n_row

    def zpeer(k):
        return (r, lax.rem(z + k, nz) * 2 + x)

    def rpeer(k):
        return (lax.rem(r + k, n_row), c)

    def rdma(src, dst, send, recv, device):
        return pltpu.make_async_remote_copy(
            src_ref=src, dst_ref=dst, send_sem=send, recv_sem=recv, device_id=device, device_id_type=MESH
        )

    class pair:
        def __init__(self, src, src_s, dst, dst_s, send, recv, device):
            self.both = (
                rdma(src, dst, send.at[0], recv.at[0], device),
                rdma(src_s, dst_s, send.at[1], recv.at[1], device),
            )

        def start(self):
            for one in self.both:
                one.start()

        def wait_send(self):
            for one in self.both:
                one.wait_send()

        def wait_recv(self):
            for one in self.both:
                one.wait_recv()

    def each(low, high, body):
        lax.fori_loop(low, high, lambda i, carry: (body(i), carry)[1], 0)

    barrier = pltpu.get_barrier_semaphore()

    def greet(device):
        pl.semaphore_signal(barrier, inc=1, device_id=device, device_id_type=MESH)

    greet(partner)
    each(1, nz, lambda k: greet(zpeer(k)))
    each(1, n_row, lambda k: greet(rpeer(k)))
    pl.semaphore_wait(barrier, 1 + (nz - 1) + (n_row - 1))

    def load(p, kind):
        if kind == "g":
            return pltpu.make_async_copy(ins[p][3], basis_g.at[p], local.at[p, 0])
        if kind == "a":
            return pltpu.make_async_copy(ins[p][2], basis_a.at[0], local.at[p, 1])
        if kind == "inputs":
            return pltpu.make_async_copy(ins[p][0], inputs_all.at[p, rows_of(c, t_col)], local.at[p, 2])
        return pltpu.make_async_copy(ins[p][1], grads_all.at[p, rows_of(r, t_row)], local.at[p, 3])

    def grads_copy(p, k, source):
        return rdma(ins[p][1], grads_all.at[p, rows_of(source, t_row)], g_send.at[p, k], g_recv.at[p, source], rpeer(k))

    def inputs_copy(p, k, source, device):
        return rdma(ins[p][0], inputs_all.at[p, rows_of(source, t_col)], i_send.at[p, k], i_recv.at[p, source], device)

    def inputs_forward(p, k, source):
        there = inputs_all.at[p, rows_of(source, t_col)]
        return rdma(there, there, f_send.at[p, k], i_recv.at[p, source], partner)

    for p in (0, 1):
        load(p, "grads").start()
        each(1, n_row, lambda k: grads_copy(p, k, r).start())
        load(p, "g").start()
        load(p, "inputs").start()
    for p in (0, 1):
        inputs_copy(p, 0, c, partner).start()
        each(1, nz, lambda k: inputs_copy(p, k, c, zpeer(k)).start())
    load(0, "a").start()

    def xcopy(p, zz):
        return pair(xsend.at[p, zz], xsend_s.at[p, zz], xrecv.at[p, zz], xrecv_s.at[p, zz],
                    xs_send.at[p, zz], xs_recv.at[p, zz], partner)

    def zcopy(p, k, slot, source):
        return pair(xrecv.at[p, slot], xrecv_s.at[p, slot], zrecv.at[p, source], zrecv_s.at[p, source],
                    zs_send.at[p, k], zs_recv.at[p, source], zpeer(k))

    def gather_copy(p, k, source, device):
        return pair(fin.at[p], fin_s.at[p], outs[p][0].at[source], outs[p][1].at[source],
                    ag_send.at[p, k], ag_recv.at[p, source], device)

    def gather_forward(p, k, source):
        return pair(outs[p][0].at[source], outs[p][1].at[source], outs[p][0].at[source], outs[p][1].at[source],
                    agf_send.at[p, k], ag_recv.at[p, source], partner)

    def acopy(p, k, slot, source):
        return pair(asend.at[p, slot], asend_s.at[p, slot], arecv.at[p, source], arecv_s.at[p, source],
                    as_send.at[p, k], as_recv.at[p, source], rpeer(k))

    def act_gather(p, k, source):
        return pair(afin.at[p], afin_s.at[p], outs[p][2].at[source], outs[p][3].at[source],
                    aa_send.at[p, k], aa_recv.at[p, source], rpeer(k))

    def put(ref, *at):
        def store(value):
            ref[at] = value

        return store

    def rotate_grads(p):
        load(p, "grads").wait()
        load(p, "g").wait()
        each(1, n_row, lambda k: grads_copy(p, k, lax.rem(r + n_row - k, n_row)).wait_recv())
        tile = min(512, width_g)

        def step(k):
            zz = lax.rem(z + k, nz)

            def columns(j):
                at = rows_of(j, tile)
                block[:, at] = jnp.dot(
                    grads_all[p, rows_of(zz, 2 * t_col), :], basis_g[p, :, at], preferred_element_type=F32
                )

            each(0, width_g // tile, columns)
            there, here = (1 - x) * (t_col // CHUNK), x * (t_col // CHUNK)

            def store(i, value):
                xsend[p, zz, rows_of(i, CHUNK), :] = value

            quantize(lambda i: block[rows_of(there + i, CHUNK), :], store, put(xsend_s, p, zz),
                     t_col // CHUNK, width_g)
            xcopy(p, zz).start()

            def keep(i):
                own[p, zz, rows_of(i, CHUNK), :] = block[rows_of(here + i, CHUNK), :]

            each(0, t_col // CHUNK, keep)

        each(0, nz, step)

    def forward_inputs(p):
        def step(k):
            source = lax.rem(z + nz - k, nz) * 2 + x
            inputs_copy(p, k, source, partner).wait_recv()
            inputs_forward(p, k, source).start()

        each(1, nz, step)

    def add_scaled(target, codes, scale, chunks):
        def step(i):
            at = rows_of(i, CHUNK)
            target[at, :] = target[at, :] + widen(codes[at, :], scale)

        each(0, chunks, step)

    def sum_x(p):
        chunks = t_col // CHUNK

        def step(k):
            zz = lax.rem(z + k, nz)
            xcopy(p, zz).wait_recv()
            add_scaled(own.at[p, zz], xrecv.at[p, zz], xrecv_s[p, zz, 0:1, 0:1], chunks)

            def store(i, value):
                xrecv[p, zz, rows_of(i, CHUNK), :] = value

            quantize(lambda i: own[p, zz, rows_of(i, CHUNK), :], store, put(xrecv_s, p, zz), chunks, width_g)
            zcopy(p, k, zz, z).start()

        each(1, nz, step)
        xcopy(p, z).wait_recv()
        add_scaled(own.at[p, z], xrecv.at[p, z], xrecv_s[p, z, 0:1, 0:1], chunks)

    def sum_z(p):
        chunks = t_col // CHUNK

        def step(k):
            source = lax.rem(z + nz - k, nz)
            zcopy(p, k, z, source).wait_recv()
            add_scaled(own.at[p, z], zrecv.at[p, source], zrecv_s[p, source, 0:1, 0:1], chunks)

        each(1, nz, step)

        def store(i, value):
            fin[p, rows_of(i, CHUNK), :] = value

        quantize(lambda i: own[p, z, rows_of(i, CHUNK), :], store, put(fin_s, p), chunks, width_g)
        gather_copy(p, 0, c, partner).start()
        each(1, nz, lambda k: gather_copy(p, k, c, zpeer(k)).start())
        pltpu.make_async_copy(fin.at[p], outs[p][0].at[c], local.at[p, 4]).start()
        pltpu.make_async_copy(fin_s.at[p], outs[p][1].at[c], local.at[p, 5]).start()

    def forward_gather(p):
        def step(k):
            source = lax.rem(z + nz - k, nz) * 2 + x
            gather_copy(p, k, source, partner).wait_recv()
            gather_forward(p, k, source).start()

        each(1, nz, step)

    def rotate_acts(p):
        load(p, "inputs").wait()
        load(p, "a").wait()
        inputs_copy(p, 0, z * 2 + 1 - x, partner).wait_recv()
        each(1, nz, lambda k: inputs_forward(p, k, lax.rem(z + nz - k, nz) * 2 + 1 - x).wait_recv())
        tile = min(512, width_a)
        chunks = t_row // CHUNK

        def rotate(piece):
            def columns(j):
                at = rows_of(j, tile)
                aown[p, :, at] = jnp.dot(
                    inputs_all[p, rows_of(piece, t_row), :], basis_a[0, :, at], preferred_element_type=F32
                )

            each(0, width_a // tile, columns)

        def step(k):
            piece = lax.rem(r + k, n_row)
            rotate(piece)

            def store(i, value):
                asend[p, k, rows_of(i, CHUNK), :] = value

            quantize(lambda i: aown[p, rows_of(i, CHUNK), :], store, put(asend_s, p, k), chunks, width_a)
            acopy(p, k, k, r).start()

        each(1, n_row, step)
        rotate(r)
        if p == 0:
            load(1, "a").start()

    def sum_acts(p):
        chunks = t_row // CHUNK

        def step(k):
            source = lax.rem(r + n_row - k, n_row)
            acopy(p, k, k, source).wait_recv()
            add_scaled(aown.at[p], arecv.at[p, source], arecv_s[p, source, 0:1, 0:1], chunks)

        each(1, n_row, step)

        def store(i, value):
            afin[p, rows_of(i, CHUNK), :] = value

        quantize(lambda i: aown[p, rows_of(i, CHUNK), :], store, put(afin_s, p), chunks, width_a)
        each(1, n_row, lambda k: act_gather(p, k, r).start())
        pltpu.make_async_copy(afin.at[p], outs[p][2].at[r], local.at[p, 6]).start()
        pltpu.make_async_copy(afin_s.at[p], outs[p][3].at[r], local.at[p, 7]).start()

    rotate_grads(0)
    forward_inputs(0)
    rotate_grads(1)
    forward_inputs(1)
    sum_x(0)
    rotate_acts(0)
    sum_z(0)
    sum_x(1)
    rotate_acts(1)
    sum_z(1)
    forward_gather(0)
    sum_acts(0)
    sum_acts(1)
    forward_gather(1)

    for p in (0, 1):
        for at, (src, dst) in enumerate(
            ((fin.at[p], outs[p][0].at[c]), (fin_s.at[p], outs[p][1].at[c]),
             (afin.at[p], outs[p][2].at[r]), (afin_s.at[p], outs[p][3].at[r]))
        ):
            pltpu.make_async_copy(src, dst, local.at[p, 4 + at]).wait()
        gather_copy(p, 0, z * 2 + 1 - x, partner).wait_recv()

        def arrivals(k):
            gather_forward(p, k, lax.rem(z + nz - k, nz) * 2 + 1 - x).wait_recv()
            gather_forward(p, k, lax.rem(z + nz - k, nz) * 2 + x).wait_send()
            inputs_forward(p, k, lax.rem(z + nz - k, nz) * 2 + x).wait_send()
            inputs_copy(p, k, c, zpeer(k)).wait_send()
            gather_copy(p, k, c, zpeer(k)).wait_send()
            zcopy(p, k, lax.rem(z + k, nz), z).wait_send()

        each(1, nz, arrivals)

        def row_arrivals(k):
            act_gather(p, k, lax.rem(r + n_row - k, n_row)).wait_recv()
            act_gather(p, k, r).wait_send()
            acopy(p, k, k, r).wait_send()
            grads_copy(p, k, r).wait_send()

        each(1, n_row, row_arrivals)
        each(0, nz, lambda zz: xcopy(p, zz).wait_send())
        inputs_copy(p, 0, c, partner).wait_send()
        gather_copy(p, 0, c, partner).wait_send()


def rotate(n_row, n_col, query, output):
    inputs, grads, act_basis, grad_basis = query
    t_col, feats_a = inputs.shape
    t_row, feats_g = grads.shape
    width_a, width_g = act_basis.shape[1], grad_basis.shape[1]
    tokens, nz = t_col * n_col, n_col // 2
    one = (
        jax.ShapeDtypeStruct((n_col, t_col, width_g), I16),
        jax.ShapeDtypeStruct((n_col, 8, 128), F32),
        jax.ShapeDtypeStruct((n_row, t_row, width_a), I16),
        jax.ShapeDtypeStruct((n_row, 8, 128), F32),
    )
    dma = pltpu.SemaphoreType.DMA
    flops = 4 * tokens * (feats_a * width_a + feats_g * width_g)
    results = pl.pallas_call(
        functools.partial(rotate_kernel, n_row, n_col),
        out_shape=one + one,
        in_specs=[pl.BlockSpec(memory_space=pl.ANY)] * 8,
        out_specs=[pl.BlockSpec(memory_space=pl.ANY)] * 8,
        scratch_shapes=[
            pltpu.VMEM((2, tokens, feats_g), BF16),
            pltpu.VMEM((2, tokens, feats_a), BF16),
            pltpu.VMEM((2, feats_g, width_g), BF16),
            pltpu.VMEM((1, feats_a, width_a), BF16),
            pltpu.VMEM((2 * t_col, width_g), F32),
            pltpu.VMEM((2, nz, t_col, width_g), F32),
            pltpu.VMEM((2, nz, t_col, width_g), I16),
            pltpu.VMEM((2, nz, 8, 128), F32),
            pltpu.VMEM((2, nz, t_col, width_g), I16),
            pltpu.VMEM((2, nz, 8, 128), F32),
            pltpu.VMEM((2, nz, t_col, width_g), I16),
            pltpu.VMEM((2, nz, 8, 128), F32),
            pltpu.VMEM((2, t_col, width_g), I16),
            pltpu.VMEM((2, 8, 128), F32),
            pltpu.VMEM((2, t_row, width_a), F32),
            pltpu.VMEM((2, n_row, t_row, width_a), I16),
            pltpu.VMEM((2, n_row, 8, 128), F32),
            pltpu.VMEM((2, n_row, t_row, width_a), I16),
            pltpu.VMEM((2, n_row, 8, 128), F32),
            pltpu.VMEM((2, t_row, width_a), I16),
            pltpu.VMEM((2, 8, 128), F32),
            dma((2, n_row)), dma((2, n_row)),
            dma((2, nz)), dma((2, nz)), dma((2, n_col)),
            dma((2, nz, 2)), dma((2, nz, 2)), dma((2, nz, 2)), dma((2, nz, 2)),
            dma((2, nz, 2)), dma((2, nz, 2)), dma((2, n_col, 2)),
            dma((2, n_row, 2)), dma((2, n_row, 2)), dma((2, n_row, 2)), dma((2, n_row, 2)),
            dma((2, 8)),
        ],
        compiler_params=pltpu.CompilerParams(
            collective_id=0, has_side_effects=True, vmem_limit_bytes=62 * 2**20
        ),
        cost_estimate=pl.CostEstimate(flops=flops, bytes_accessed=32 * 2**20, transcendentals=0),
        name="rotate",
    )(*query, *output)
    return results[:4], results[4:]


def product_kernel(depth, starts, g_ref, gs_ref, a_ref, as_ref, out_ref, a_cat, g_raw, acc):
    blocks = a_ref.shape[0] // depth

    @pl.when(pl.program_id(0) == 0)
    def _():
        for b in range(blocks):
            at = pl.ds(b * depth, depth)
            value = widen(a_ref[at, :], as_ref[at, :])
            high = value.astype(BF16)
            low = (value - high.astype(F32)).astype(BF16)
            a_cat[b, pl.ds(0, depth), :] = high
            a_cat[b, pl.ds(depth, depth), :] = low
            a_cat[b, pl.ds(2 * depth, depth), :] = high

    for b in range(blocks):
        at = pl.ds(b * depth, depth)
        g_raw[b] = widen(g_ref[at, :], gs_ref[at, :])

    for s in range(SEQS):
        low_token, high_token = starts[s], starts[s + 1]
        acc[...] = jnp.zeros_like(acc)
        for b in range(blocks):

            @pl.when((low_token < (b + 1) * depth) & (high_token > b * depth))
            def _():
                place = lax.broadcasted_iota(I32, (depth, 1), 0) + b * depth
                value = jnp.where((place >= low_token) & (place < high_token), g_raw[b], 0.0)
                high = value.astype(BF16)
                low = (value - high.astype(F32)).astype(BF16)
                both = jnp.concatenate([high, high, low], axis=0)
                acc[...] += lax.dot_general(
                    both, a_cat[b], (((0,), (0,)), ((), ())), preferred_element_type=F32
                )

        if s == 0:
            out_ref[...] = acc[...] * acc[...]
        elif s < SEQS - 1:
            out_ref[...] += acc[...] * acc[...]
        else:
            out_ref[...] = (out_ref[...] + acc[...] * acc[...]) * (1.0 / SEQS)


def correct(starts, g, g_scale, a, a_scale):
    tokens = g.shape[0] * g.shape[1]
    gs = jnp.repeat(g_scale[:, 0, 0], g.shape[1])[:, None]
    acts = jnp.repeat(a_scale[:, 0, 0], a.shape[1])[:, None]
    g, a = g.reshape(tokens, -1), a.reshape(tokens, -1)
    width_g, width_a = g.shape[1], a.shape[1]
    depth, tile = min(256, tokens), min(512, width_g)
    blocks = tokens // depth
    return pl.pallas_call(
        functools.partial(product_kernel, depth),
        out_shape=jax.ShapeDtypeStruct((width_g, width_a), F32),
        grid_spec=pltpu.PrefetchScalarGridSpec(
            num_scalar_prefetch=1,
            grid=(width_g // tile,),
            in_specs=[
                pl.BlockSpec((tokens, tile), lambda i, s: (0, i)),
                pl.BlockSpec((tokens, 1), lambda i, s: (0, 0)),
                pl.BlockSpec((tokens, width_a), lambda i, s: (0, 0)),
                pl.BlockSpec((tokens, 1), lambda i, s: (0, 0)),
            ],
            out_specs=pl.BlockSpec((tile, width_a), lambda i, s: (i, 0)),
            scratch_shapes=[
                pltpu.VMEM((blocks, 3 * depth, width_a), BF16),
                pltpu.VMEM((blocks, depth, tile), F32),
                pltpu.VMEM((tile, width_a), F32),
            ],
        ),
        compiler_params=pltpu.CompilerParams(vmem_limit_bytes=56 * 2**20),
        cost_estimate=pl.CostEstimate(
            flops=2 * 6 * 7 * depth * width_g * width_a // 2, bytes_accessed=16 * 2**20, transcendentals=0
        ),
        name="correct",
    )(starts, g, gs, a, acts)


def per_device(n_row, n_col, seq_ids, *args):
    bounds = jnp.arange(SEQS + 1, dtype=I32)
    starts = jnp.sum((seq_ids[None, :] < bounds[:, None]).astype(I32), axis=1)
    query, output = rotate(n_row, n_col, args[:4], args[4:])
    return correct(starts, *query), correct(starts, *output)


def solution(mesh):
    one = (P("col", "row"), P("row", "col"), P("row", "col"), P("col", "row"))
    return jax.shard_map(
        functools.partial(per_device, mesh.shape["row"], mesh.shape["col"]),
        mesh=mesh,
        in_specs=(P(),) + one + one,
        out_specs=(P("row", "col"), P("row", "col")),
        check_vma=False,
    )
```

```python
import functools

import jax
import jax.numpy as jnp
from jax import lax
from jax.experimental import pallas as pl
from jax.experimental.pallas import tpu as pltpu
from jax.sharding import PartitionSpec as P

SEQS = 4
CHUNK = 16
TOP = 32767.0
MESH = pl.DeviceIdType.MESH
F32, BF16, I16, I32 = jnp.float32, jnp.bfloat16, jnp.int16, jnp.int32


def quantize(load, store, store_scale, chunks, width):
    most = lax.fori_loop(
        0, chunks, lambda i, m: jnp.maximum(m, jnp.abs(load(i))), jnp.zeros((CHUNK, width), F32)
    )
    most = jnp.max(jnp.max(most, axis=1, keepdims=True), axis=0, keepdims=True)
    inverse = jnp.where(most > 1e-30, TOP / jnp.maximum(most, 1e-30), 0.0)
    store_scale(jnp.broadcast_to(most * (1.0 / TOP), (8, 128)))

    def body(i, carry):
        store(i, jnp.round(load(i) * inverse).astype(I32).astype(I16))
        return carry

    lax.fori_loop(0, chunks, body, 0)


def widen(codes, scale):
    return codes.astype(I32).astype(F32) * scale


def rows_of(i, size):
    return pl.ds(pl.multiple_of(i * size, size), size)


def rotate_kernel(n_row, n_col, depth, tile_g, parts, marks, flags, masks, *refs):
    ins, refs = (refs[0:4], refs[4:8]), refs[8:]
    outs, refs = (refs[0:5], refs[5:10]), refs[10:]
    (grads_all, inputs_all, basis_g, basis_a, block, own, xsend, xsend_s, xrecv, xrecv_s, zrecv, zrecv_s,
     fin, fin_s, aown, asend, asend_s, arecv, arecv_s, afin, afin_s,
     codes, codes_s, turned, acc, stage,
     g_send, g_recv, i_send, f_send, i_recv, xs_send, xs_recv, zs_send, zs_recv,
     ag_send, agf_send, ag_recv, as_send, as_recv, aa_send, aa_recv, local, codes_sem, stage_sem) = refs

    r, c = lax.axis_index("row"), lax.axis_index("col")
    nz = n_col // 2
    z, x = c // 2, lax.rem(c, 2)
    partner = (r, z * 2 + 1 - x)
    tokens = grads_all.shape[1] * grads_all.shape[2]
    feats_a = basis_a.shape[1]
    width_g, width_a = basis_g.shape[2], basis_a.shape[2]
    t_col, t_row = tokens // n_col, tokens // n_row

    def zpeer(k):
        return (r, lax.rem(z + k, nz) * 2 + x)

    def rpeer(k):
        return (lax.rem(r + k, n_row), c)

    def rdma(src, dst, send, recv, device):
        return pltpu.make_async_remote_copy(
            src_ref=src, dst_ref=dst, send_sem=send, recv_sem=recv, device_id=device, device_id_type=MESH
        )

    class pair:
        def __init__(self, src, src_s, dst, dst_s, send, recv, device):
            self.both = (
                rdma(src, dst, send.at[0], recv.at[0], device),
                rdma(src_s, dst_s, send.at[1], recv.at[1], device),
            )

        def start(self):
            for one in self.both:
                one.start()

        def wait_send(self):
            for one in self.both:
                one.wait_send()

        def wait_recv(self):
            for one in self.both:
                one.wait_recv()

    def each(low, high, body):
        lax.fori_loop(low, high, lambda i, carry: (body(i), carry)[1], 0)

    barrier = pltpu.get_barrier_semaphore()

    def greet(device):
        pl.semaphore_signal(barrier, inc=1, device_id=device, device_id_type=MESH)

    greet(partner)
    each(1, nz, lambda k: greet(zpeer(k)))
    each(1, n_row, lambda k: greet(rpeer(k)))
    pl.semaphore_wait(barrier, 1 + (nz - 1) + (n_row - 1))

    def place(i, size):
        runs = depth // size
        return lax.div(i, runs), rows_of(lax.rem(i, runs), size)

    def load(p, kind):
        if kind == "g":
            return pltpu.make_async_copy(ins[p][3], basis_g.at[0], local.at[p, 0])
        if kind == "a":
            return pltpu.make_async_copy(ins[p][2], basis_a.at[0], local.at[p, 1])
        if kind == "inputs":
            return pltpu.make_async_copy(ins[p][0], inputs_all.at[p, rows_of(c, t_col)], local.at[p, 2])
        return pltpu.make_async_copy(ins[p][1], grads_all.at[p, *place(r, t_row)], local.at[p, 3])

    def grads_copy(p, k, source):
        return rdma(ins[p][1], grads_all.at[p, *place(source, t_row)], g_send.at[p, k], g_recv.at[p, source], rpeer(k))

    def inputs_copy(p, k, source, device):
        return rdma(ins[p][0], inputs_all.at[p, rows_of(source, t_col)], i_send.at[p, k], i_recv.at[p, source], device)

    def inputs_forward(p, k, source):
        there = inputs_all.at[p, rows_of(source, t_col)]
        return rdma(there, there, f_send.at[p, k], i_recv.at[p, source], partner)

    def start_grads(p):
        load(p, "grads").start()
        each(1, n_row, lambda k: grads_copy(p, k, r).start())

    def start_inputs(p):
        load(p, "inputs").start()
        inputs_copy(p, 0, c, partner).start()
        each(1, nz, lambda k: inputs_copy(p, k, c, zpeer(k)).start())

    start_grads(0)
    start_inputs(0)
    load(0, "g").start()
    load(0, "a").start()

    def xcopy(p, zz):
        return pair(xsend.at[p, zz], xsend_s.at[p, zz], xrecv.at[p, zz], xrecv_s.at[p, zz],
                    xs_send.at[p, zz], xs_recv.at[p, zz], partner)

    def zcopy(p, k, slot):
        return pair(xrecv.at[p, slot], xrecv_s.at[p, slot], zrecv.at[p, k - 1], zrecv_s.at[p, k - 1],
                    zs_send.at[p, k], zs_recv.at[p, k], zpeer(k))

    part = width_g // parts

    def columns_of(q):
        return pl.ds(pl.multiple_of(q * part, part), part)

    def gather_copy(p, q, k, source, device):
        return rdma(fin.at[p, :, columns_of(q)], outs[p][0].at[source, :, columns_of(q)],
                    ag_send.at[p, k, q], ag_recv.at[p, source, q], device)

    def gather_forward(p, q, k, source):
        there = outs[p][0].at[source, :, columns_of(q)]
        return rdma(there, there, agf_send.at[p, k, q], ag_recv.at[p, source, q], partner)

    def scale_copy(p, k, source, device):
        return rdma(fin_s.at[p], outs[p][1].at[source], ag_send.at[p, k, parts], ag_recv.at[p, source, parts], device)

    def scale_forward(p, k, source):
        there = outs[p][1].at[source]
        return rdma(there, there, agf_send.at[p, k, parts], ag_recv.at[p, source, parts], partner)

    def acopy(p, k, slot, source):
        return pair(asend.at[p, slot], asend_s.at[p, slot], arecv.at[p, source], arecv_s.at[p, source],
                    as_send.at[p, k], as_recv.at[p, source], rpeer(k))

    def act_gather(p, k, source):
        return pair(afin.at[p], afin_s.at[p], outs[p][2].at[source], outs[p][3].at[source],
                    aa_send.at[p, k], aa_recv.at[p, source], rpeer(k))

    def put(ref, *at):
        def store(value):
            ref[at] = value

        return store

    def rotate_grads(p):
        load(p, "grads").wait()
        load(p, "g").wait()
        each(1, n_row, lambda k: grads_copy(p, k, lax.rem(r + n_row - k, n_row)).wait_recv())
        if p == 0:
            start_grads(1)
        tile = min(512, width_g)

        def step(k):
            zz = lax.rem(z + k, nz)

            def columns(j):
                at = rows_of(j, tile)
                block[:, at] = jnp.dot(
                    grads_all[p, *place(zz, 2 * t_col), :], basis_g[0, :, at], preferred_element_type=F32
                )

            each(0, width_g // tile, columns)
            there, here = (1 - x) * (t_col // CHUNK), x * (t_col // CHUNK)

            def store(i, value):
                xsend[p, zz, rows_of(i, CHUNK), :] = value

            quantize(lambda i: block[rows_of(there + i, CHUNK), :], store, put(xsend_s, p, zz),
                     t_col // CHUNK, width_g)
            xcopy(p, zz).start()

            def keep(i):
                own[p, zz, rows_of(i, CHUNK), :] = block[rows_of(here + i, CHUNK), :]

            each(0, t_col // CHUNK, keep)

        each(0, nz, step)
        if p == 0:
            load(1, "g").start()
            start_inputs(1)

    def forward_inputs(p):
        def step(k):
            source = lax.rem(z + nz - k, nz) * 2 + x
            inputs_copy(p, k, source, partner).wait_recv()
            inputs_forward(p, k, source).start()

        each(1, nz, step)

    def add_scaled(target, codes, scale, chunks):
        def step(i):
            at = rows_of(i, CHUNK)
            target[at, :] = target[at, :] + widen(codes[at, :], scale)

        each(0, chunks, step)

    def sum_x(p):
        chunks = t_col // CHUNK

        def step(k):
            zz = lax.rem(z + k, nz)
            xcopy(p, zz).wait_recv()
            add_scaled(own.at[p, zz], xrecv.at[p, zz], xrecv_s[p, zz, 0:1, 0:1], chunks)

            def store(i, value):
                xrecv[p, zz, rows_of(i, CHUNK), :] = value

            quantize(lambda i: own[p, zz, rows_of(i, CHUNK), :], store, put(xrecv_s, p, zz), chunks, width_g)
            zcopy(p, k, zz).start()

        each(1, nz, step)
        xcopy(p, z).wait_recv()
        add_scaled(own.at[p, z], xrecv.at[p, z], xrecv_s[p, z, 0:1, 0:1], chunks)

    def sum_z(p):
        chunks = t_col // CHUNK

        def step(k):
            zcopy(p, k, z).wait_recv()
            add_scaled(own.at[p, z], zrecv.at[p, k - 1], zrecv_s[p, k - 1, 0:1, 0:1], chunks)

        each(1, nz, step)

        def store(i, value):
            fin[p, rows_of(i, CHUNK), :] = value

        quantize(lambda i: own[p, z, rows_of(i, CHUNK), :], store, put(fin_s, p), chunks, width_g)
        scale_copy(p, 0, c, partner).start()
        each(1, nz, lambda k: scale_copy(p, k, c, zpeer(k)).start())

        def push(q):
            each(1, nz, lambda k: gather_copy(p, q, k, c, zpeer(k)).start())
            gather_copy(p, q, 0, c, partner).start()

        each(0, parts, push)
        pltpu.make_async_copy(fin.at[p], outs[p][0].at[c], local.at[p, 4]).start()
        pltpu.make_async_copy(fin_s.at[p], outs[p][1].at[c], local.at[p, 5]).start()

    def forward_scales(p):
        def step(k):
            source = lax.rem(z + nz - k, nz) * 2 + x
            scale_copy(p, k, source, partner).wait_recv()
            scale_forward(p, k, source).start()

        each(1, nz, step)

    def forward_gather(p, q):
        def step(k):
            source = lax.rem(z + nz - k, nz) * 2 + x
            gather_copy(p, q, k, source, partner).wait_recv()
            gather_forward(p, q, k, source).start()

        each(1, nz, step)

    def rotate_acts(p):
        load(p, "inputs").wait()
        load(p, "a").wait()
        inputs_copy(p, 0, z * 2 + 1 - x, partner).wait_recv()
        each(1, nz, lambda k: inputs_forward(p, k, lax.rem(z + nz - k, nz) * 2 + 1 - x).wait_recv())
        tile = min(512, width_a)
        chunks = t_row // CHUNK

        def rotate(piece):
            def columns(j):
                at = rows_of(j, tile)
                aown[p, :, at] = jnp.dot(
                    inputs_all[p, rows_of(piece, t_row), :], basis_a[0, :, at], preferred_element_type=F32
                )

            each(0, width_a // tile, columns)

        def step(k):
            piece = lax.rem(r + k, n_row)
            rotate(piece)

            def store(i, value):
                asend[p, k - 1, rows_of(i, CHUNK), :] = value

            quantize(lambda i: aown[p, rows_of(i, CHUNK), :], store, put(asend_s, p, k - 1), chunks, width_a)
            acopy(p, k, k - 1, r).start()

        each(1, n_row, step)
        rotate(r)
        if p == 0:
            load(1, "a").start()

    def sum_acts(p):
        chunks = t_row // CHUNK

        def step(k):
            source = lax.rem(r + n_row - k, n_row)
            acopy(p, k, k - 1, source).wait_recv()
            add_scaled(aown.at[p], arecv.at[p, source], arecv_s[p, source, 0:1, 0:1], chunks)

        each(1, n_row, step)

        def store(i, value):
            afin[p, rows_of(i, CHUNK), :] = value

        quantize(lambda i: aown[p, rows_of(i, CHUNK), :], store, put(afin_s, p), chunks, width_a)
        each(1, n_row, lambda k: act_gather(p, k, r).start())
        pltpu.make_async_copy(afin.at[p], outs[p][2].at[r], local.at[p, 6]).start()
        pltpu.make_async_copy(afin_s.at[p], outs[p][3].at[r], local.at[p, 7]).start()

    def own_copies(p):
        return [
            pltpu.make_async_copy(src, dst, local.at[p, 4 + at])
            for at, (src, dst) in enumerate(
                ((fin.at[p], outs[p][0].at[c]), (fin_s.at[p], outs[p][1].at[c]),
                 (afin.at[p], outs[p][2].at[r]), (afin_s.at[p], outs[p][3].at[r]))
            )
        ]

    blocks, per_block = tokens // depth, depth // t_col

    def prepare(p):
        for one in own_copies(p):
            one.wait()
        each(1, n_row, lambda k: act_gather(p, k, lax.rem(r + n_row - k, n_row)).wait_recv())
        both = (
            pltpu.make_async_copy(outs[p][2], arecv.at[p], codes_sem.at[0]),
            pltpu.make_async_copy(outs[p][3], arecv_s.at[p], codes_sem.at[1]),
        )
        for one in both:
            one.start()
        for one in both:
            one.wait()

        def split(piece):
            def step(i):
                value = widen(arecv[p, piece, rows_of(i, CHUNK), :], arecv_s[p, piece, 0:1, 0:1])
                high = value.astype(BF16)
                block_of, rows = place(piece * (t_row // CHUNK) + i, CHUNK)
                grads_all[0, block_of, rows, :] = high
                grads_all[1, block_of, rows, :] = (value - high.astype(F32)).astype(BF16)

            each(0, t_row // CHUNK, step)

        each(0, n_row, split)

    def arrived_scales(p):
        scale_copy(p, 0, z * 2 + 1 - x, partner).wait_recv()
        each(1, nz, lambda k: scale_forward(p, k, lax.rem(z + nz - k, nz) * 2 + 1 - x).wait_recv())
        copy = pltpu.make_async_copy(outs[p][1], codes_s, codes_sem.at[1])
        copy.start()
        copy.wait()

    def arrived(p, q):
        gather_copy(p, q, 0, z * 2 + 1 - x, partner).wait_recv()
        each(1, nz, lambda k: gather_forward(p, q, k, lax.rem(z + nz - k, nz) * 2 + 1 - x).wait_recv())

    def write(p, j):
        slot = lax.rem(j, 2)
        return pltpu.make_async_copy(stage.at[slot], outs[p][4].at[rows_of(j, tile_g)], stage_sem.at[slot])

    def multiply(m):
        b = marks[m]
        inside = masks[m, 0:1, :].astype(BF16)
        high, low = turned[b, :, pl.ds(0, depth)] * inside, turned[b, :, pl.ds(depth, depth)] * inside
        a_high, a_low = grads_all[0, b], grads_all[1, b]
        return jnp.dot(
            jnp.concatenate([high, high, low], axis=1),
            jnp.concatenate([a_high, a_low, a_high], axis=0),
            preferred_element_type=F32,
        )

    def product(p, j):
        copy = pltpu.make_async_copy(outs[p][0].at[:, :, rows_of(j, tile_g)], codes, codes_sem.at[0])
        copy.start()
        copy.wait()
        for b in range(blocks):
            at = pl.ds(b * per_block, per_block)
            value = widen(codes[at], codes_s[at, 0:1, 0:1]).reshape(depth, tile_g)
            high = value.astype(BF16)
            turned[b, :, pl.ds(0, depth)] = high.T
            turned[b, :, pl.ds(depth, depth)] = (value - high.astype(F32)).astype(BF16).T

        @pl.when(j >= 2)
        def _():
            write(p, j - 2).wait()

        slot = lax.rem(j, 2)
        acc[...] = multiply(0)
        stage[slot] = acc[...] * acc[...] * flags[1, 0]

        def step(m):
            acc[...] = acc[...] * flags[0, m] + multiply(m)
            stage[slot] = stage[slot] + acc[...] * acc[...] * flags[1, m]

        each(1, marks.shape[0], step)
        write(p, j).start()

    tiles, per_part = width_g // tile_g, part // tile_g

    rotate_grads(0)
    forward_inputs(0)
    rotate_grads(1)
    sum_x(0)
    rotate_acts(0)
    forward_inputs(1)
    sum_z(0)
    sum_x(1)
    sum_acts(0)
    rotate_acts(1)
    forward_scales(0)
    each(0, parts, lambda q: forward_gather(0, q))
    sum_z(1)
    sum_acts(1)
    prepare(0)
    arrived_scales(0)
    forward_scales(1)

    def overlap(q):
        arrived(0, q)
        each(q * per_part, (q + 1) * per_part, lambda j: product(0, j))
        forward_gather(1, q)

    def last(q):
        arrived(1, q)
        each(q * per_part, (q + 1) * per_part, lambda j: product(1, j))

    def drain(p):
        for j in range(max(0, tiles - 2), tiles):
            write(p, j).wait()

    each(0, parts, overlap)
    drain(0)
    prepare(1)
    arrived_scales(1)
    each(0, parts, last)
    drain(1)

    for p in (0, 1):

        def departures(k):
            source = lax.rem(z + nz - k, nz) * 2 + x
            scale_forward(p, k, source).wait_send()
            scale_copy(p, k, c, zpeer(k)).wait_send()
            each(0, parts, lambda q: gather_forward(p, q, k, source).wait_send())
            each(0, parts, lambda q: gather_copy(p, q, k, c, zpeer(k)).wait_send())
            inputs_copy(p, k, c, zpeer(k)).wait_send()
            inputs_forward(p, k, source).wait_send()
            zcopy(p, k, lax.rem(z + k, nz)).wait_send()

        each(1, nz, departures)

        def row_departures(k):
            act_gather(p, k, r).wait_send()
            acopy(p, k, k - 1, r).wait_send()
            grads_copy(p, k, r).wait_send()

        each(1, n_row, row_departures)
        each(0, nz, lambda zz: xcopy(p, zz).wait_send())
        inputs_copy(p, 0, c, partner).wait_send()
        scale_copy(p, 0, c, partner).wait_send()
        each(0, parts, lambda q: gather_copy(p, q, 0, c, partner).wait_send())


def segments(seq_ids, tokens, depth):
    starts = jnp.sum((seq_ids[None, :] < jnp.arange(1, SEQS, dtype=I32)[:, None]).astype(I32), axis=1)
    cuts = jnp.sort(jnp.concatenate([starts, jnp.arange(depth, tokens, depth, dtype=I32)]))
    low = jnp.concatenate([jnp.zeros((1,), I32), cuts])
    high = jnp.concatenate([cuts, jnp.full((1,), tokens, I32)])
    block = jnp.minimum(low // depth, tokens // depth - 1)
    numbers = jnp.sum((starts[None, :] <= low[:, None]).astype(I32), axis=1)
    same = (numbers[1:] == numbers[:-1]).astype(F32)
    goes_on = jnp.concatenate([jnp.zeros((1,), F32), same])
    ends = jnp.concatenate([1.0 - same, jnp.ones((1,), F32)]) / SEQS
    tokens_of = block[:, None] * depth + jnp.arange(depth, dtype=I32)[None, :]
    inside = ((tokens_of >= low[:, None]) & (tokens_of < high[:, None])).astype(F32)
    return block, jnp.stack([goes_on, ends]), jnp.repeat(inside[:, None, :], 8, axis=1)


def rotate(n_row, n_col, seq_ids, query, output):
    inputs, grads, act_basis, grad_basis = query
    t_col, feats_a = inputs.shape
    t_row, feats_g = grads.shape
    width_a, width_g = act_basis.shape[1], grad_basis.shape[1]
    tokens, nz = t_col * n_col, n_col // 2
    one = (
        jax.ShapeDtypeStruct((n_col, t_col, width_g), I16),
        jax.ShapeDtypeStruct((n_col, 8, 128), F32),
        jax.ShapeDtypeStruct((n_row, t_row, width_a), I16),
        jax.ShapeDtypeStruct((n_row, 8, 128), F32),
        jax.ShapeDtypeStruct((width_g, width_a), F32),
    )
    depth, tile_g = min(256, tokens), min(256, width_g)
    parts = max(1, min(4, width_g // tile_g))
    marks, flags, masks = segments(seq_ids, tokens, depth)
    dma = pltpu.SemaphoreType.DMA
    flops = 4 * tokens * (feats_a * width_a + feats_g * width_g + 6 * width_g * width_a)
    results = pl.pallas_call(
        functools.partial(rotate_kernel, n_row, n_col, depth, tile_g, parts),
        out_shape=one + one,
        in_specs=[pl.BlockSpec(memory_space=pltpu.SMEM)] * 2
        + [pl.BlockSpec(memory_space=pltpu.VMEM)]
        + [pl.BlockSpec(memory_space=pl.ANY)] * 8,
        out_specs=[pl.BlockSpec(memory_space=pl.ANY)] * 10,
        scratch_shapes=[
            pltpu.VMEM((2, tokens // depth, depth, feats_g), BF16),
            pltpu.VMEM((2, tokens, feats_a), BF16),
            pltpu.VMEM((1, feats_g, width_g), BF16),
            pltpu.VMEM((1, feats_a, width_a), BF16),
            pltpu.VMEM((2 * t_col, width_g), F32),
            pltpu.VMEM((2, nz, t_col, width_g), F32),
            pltpu.VMEM((2, nz, t_col, width_g), I16),
            pltpu.VMEM((2, nz, 8, 128), F32),
            pltpu.VMEM((2, nz, t_col, width_g), I16),
            pltpu.VMEM((2, nz, 8, 128), F32),
            pltpu.VMEM((2, nz - 1, t_col, width_g), I16),
            pltpu.VMEM((2, nz - 1, 8, 128), F32),
            pltpu.VMEM((2, t_col, width_g), I16),
            pltpu.VMEM((2, 8, 128), F32),
            pltpu.VMEM((2, t_row, width_a), F32),
            pltpu.VMEM((2, n_row - 1, t_row, width_a), I16),
            pltpu.VMEM((2, n_row - 1, 8, 128), F32),
            pltpu.VMEM((2, n_row, t_row, width_a), I16),
            pltpu.VMEM((2, n_row, 8, 128), F32),
            pltpu.VMEM((2, t_row, width_a), I16),
            pltpu.VMEM((2, 8, 128), F32),
            pltpu.VMEM((n_col, t_col, tile_g), I16),
            pltpu.VMEM((n_col, 8, 128), F32),
            pltpu.VMEM((tokens // depth, tile_g, 2 * depth), BF16),
            pltpu.VMEM((tile_g, width_a), F32),
            pltpu.VMEM((2, tile_g, width_a), F32),
            dma((2, n_row)), dma((2, n_row)),
            dma((2, nz)), dma((2, nz)), dma((2, n_col)),
            dma((2, nz, 2)), dma((2, nz, 2)), dma((2, nz, 2)), dma((2, nz, 2)),
            dma((2, nz, parts + 1)), dma((2, nz, parts + 1)), dma((2, n_col, parts + 1)),
            dma((2, n_row, 2)), dma((2, n_row, 2)), dma((2, n_row, 2)), dma((2, n_row, 2)),
            dma((2, 8)), dma((2,)), dma((2,)),
        ],
        compiler_params=pltpu.CompilerParams(
            collective_id=0, has_side_effects=True, vmem_limit_bytes=62 * 2**20
        ),
        cost_estimate=pl.CostEstimate(flops=flops, bytes_accessed=32 * 2**20, transcendentals=0),
        name="rotate",
    )(marks, flags, masks, *query, *output)
    return results[4], results[9]


def per_device(n_row, n_col, seq_ids, *args):
    return rotate(n_row, n_col, seq_ids, args[:4], args[4:])


def solution(mesh):
    one = (P("col", "row"), P("row", "col"), P("row", "col"), P("col", "row"))
    return jax.shard_map(
        functools.partial(per_device, mesh.shape["row"], mesh.shape["col"]),
        mesh=mesh,
        in_specs=(P(),) + one + one,
        out_specs=(P("row", "col"), P("row", "col")),
        check_vma=False,
    )
```

```python
import functools

import jax
import jax.numpy as jnp
from jax import lax
from jax.experimental import pallas as pl
from jax.experimental.pallas import tpu as pltpu
from jax.sharding import PartitionSpec as P

SEQS = 4
CHUNK = 16
TOP = 32767.0
MESH = pl.DeviceIdType.MESH
F32, BF16, I16, I32 = jnp.float32, jnp.bfloat16, jnp.int16, jnp.int32


def quantize(load, store, store_scale, chunks, width):
    most = lax.fori_loop(
        0, chunks, lambda i, m: jnp.maximum(m, jnp.abs(load(i))), jnp.zeros((CHUNK, width), F32)
    )
    most = jnp.max(jnp.max(most, axis=1, keepdims=True), axis=0, keepdims=True)
    inverse = jnp.where(most > 1e-30, TOP / jnp.maximum(most, 1e-30), 0.0)
    store_scale(jnp.broadcast_to(most * (1.0 / TOP), (8, 128)))

    def body(i, carry):
        store(i, jnp.round(load(i) * inverse).astype(I32).astype(I16))
        return carry

    lax.fori_loop(0, chunks, body, 0)


def widen(codes, scale):
    return codes.astype(I32).astype(F32) * scale


def rows_of(i, size):
    return pl.ds(pl.multiple_of(i * size, size), size)


def rotate_kernel(n_row, n_col, depth, tile_g, parts, marks, flags, masks, *refs):
    ins, refs = (refs[0:4], refs[4:8]), refs[8:]
    outs, refs = (refs[0:5], refs[5:10]), refs[10:]
    (grads_all, inputs_all, basis_g, basis_a, block, own, xsend, xsend_s, xrecv, xrecv_s, zrecv, zrecv_s,
     fin_s, aown, asend, asend_s, arecv, arecv_s, afin, afin_s,
     codes, codes_s, turned, acc, stage,
     g_send, g_recv, i_send, f_send, i_recv, xs_send, xs_recv, zs_send, zs_recv,
     ag_send, agf_send, ag_recv, as_send, as_recv, aa_send, aa_recv, local, codes_sem, stage_sem) = refs

    r, c = lax.axis_index("row"), lax.axis_index("col")
    nz = n_col // 2
    z, x = c // 2, lax.rem(c, 2)
    partner = (r, z * 2 + 1 - x)
    tokens = grads_all.shape[1] * grads_all.shape[2]
    feats_a = basis_a.shape[1]
    width_g, width_a = basis_g.shape[2], basis_a.shape[2]
    t_col, t_row = tokens // n_col, tokens // n_row

    def zpeer(k):
        return (r, lax.rem(z + k, nz) * 2 + x)

    def rpeer(k):
        return (lax.rem(r + k, n_row), c)

    def rdma(src, dst, send, recv, device):
        return pltpu.make_async_remote_copy(
            src_ref=src, dst_ref=dst, send_sem=send, recv_sem=recv, device_id=device, device_id_type=MESH
        )

    class pair:
        def __init__(self, src, src_s, dst, dst_s, send, recv, device):
            self.both = (
                rdma(src, dst, send.at[0], recv.at[0], device),
                rdma(src_s, dst_s, send.at[1], recv.at[1], device),
            )

        def start(self):
            for one in self.both:
                one.start()

        def wait_send(self):
            for one in self.both:
                one.wait_send()

        def wait_recv(self):
            for one in self.both:
                one.wait_recv()

    def each(low, high, body):
        lax.fori_loop(low, high, lambda i, carry: (body(i), carry)[1], 0)

    barrier = pltpu.get_barrier_semaphore()

    def greet(device):
        pl.semaphore_signal(barrier, inc=1, device_id=device, device_id_type=MESH)

    greet(partner)
    each(1, nz, lambda k: greet(zpeer(k)))
    each(1, n_row, lambda k: greet(rpeer(k)))
    pl.semaphore_wait(barrier, 1 + (nz - 1) + (n_row - 1))

    def place(i, size):
        runs = depth // size
        return lax.div(i, runs), rows_of(lax.rem(i, runs), size)

    def load(p, kind):
        if kind == "g":
            return pltpu.make_async_copy(ins[p][3], basis_g.at[0], local.at[p, 0])
        if kind == "a":
            return pltpu.make_async_copy(ins[p][2], basis_a.at[0], local.at[p, 1])
        if kind == "inputs":
            return pltpu.make_async_copy(ins[p][0], inputs_all.at[p, rows_of(c, t_col)], local.at[p, 2])
        return pltpu.make_async_copy(ins[p][1], grads_all.at[p, *place(r, t_row)], local.at[p, 3])

    def grads_copy(p, k, source):
        return rdma(ins[p][1], grads_all.at[p, *place(source, t_row)], g_send.at[p, k], g_recv.at[p, source], rpeer(k))

    def inputs_copy(p, k, source, device):
        return rdma(ins[p][0], inputs_all.at[p, rows_of(source, t_col)], i_send.at[p, k], i_recv.at[p, source], device)

    def inputs_forward(p, k, source):
        there = inputs_all.at[p, rows_of(source, t_col)]
        return rdma(there, there, f_send.at[p, k], i_recv.at[p, source], partner)

    def start_grads(p):
        load(p, "grads").start()
        each(1, n_row, lambda k: grads_copy(p, k, r).start())

    def start_inputs(p):
        load(p, "inputs").start()
        each(1, nz, lambda k: inputs_copy(p, k, c, zpeer(k)).start())

    start_grads(0)
    start_inputs(0)
    inputs_copy(0, 0, c, partner).start()
    inputs_copy(1, 0, c, partner).start()
    load(0, "g").start()
    load(0, "a").start()

    def xcopy(p, zz):
        return pair(xsend.at[p, zz], xsend_s.at[p, zz], xrecv.at[p, zz], xrecv_s.at[p, zz],
                    xs_send.at[p, zz], xs_recv.at[p, zz], partner)

    def zcopy(p, k, slot):
        return pair(xrecv.at[p, slot], xrecv_s.at[p, slot], zrecv.at[p, k - 1], zrecv_s.at[p, k - 1],
                    zs_send.at[p, k], zs_recv.at[p, k], zpeer(k))

    part = width_g // parts

    def columns_of(q):
        return pl.ds(pl.multiple_of(q * part, part), part)

    def gather_copy(p, q, k, source, device):
        return rdma(xrecv.at[p, z, :, columns_of(q)], outs[p][0].at[source, :, columns_of(q)],
                    ag_send.at[p, k, q], ag_recv.at[p, source, q], device)

    def gather_forward(p, q, k, source):
        there = outs[p][0].at[source, :, columns_of(q)]
        return rdma(there, there, agf_send.at[p, k, q], ag_recv.at[p, source, q], partner)

    def scale_copy(p, k, source, device):
        return rdma(fin_s.at[p], outs[p][1].at[source], ag_send.at[p, k, parts], ag_recv.at[p, source, parts], device)

    def scale_forward(p, k, source):
        there = outs[p][1].at[source]
        return rdma(there, there, agf_send.at[p, k, parts], ag_recv.at[p, source, parts], partner)

    def acopy(p, k, slot, source):
        return pair(asend.at[p, slot], asend_s.at[p, slot], arecv.at[p, source], arecv_s.at[p, source],
                    as_send.at[p, k], as_recv.at[p, source], rpeer(k))

    def act_gather(p, k, source):
        return pair(afin.at[p], afin_s.at[p], outs[p][2].at[source], outs[p][3].at[source],
                    aa_send.at[p, k], aa_recv.at[p, source], rpeer(k))

    def put(ref, *at):
        def store(value):
            ref[at] = value

        return store

    def rotate_grads(p):
        load(p, "grads").wait()
        load(p, "g").wait()
        each(1, n_row, lambda k: grads_copy(p, k, lax.rem(r + n_row - k, n_row)).wait_recv())
        if p == 0:
            start_grads(1)
        tile = min(512, width_g)

        def step(k):
            zz = lax.rem(z + k, nz)

            def columns(j):
                at = rows_of(j, tile)
                block[:, at] = jnp.dot(
                    grads_all[p, *place(zz, 2 * t_col), :], basis_g[0, :, at], preferred_element_type=F32
                )

            each(0, width_g // tile, columns)
            there, here = (1 - x) * (t_col // CHUNK), x * (t_col // CHUNK)

            def store(i, value):
                xsend[p, zz, rows_of(i, CHUNK), :] = value

            quantize(lambda i: block[rows_of(there + i, CHUNK), :], store, put(xsend_s, p, zz),
                     t_col // CHUNK, width_g)
            xcopy(p, zz).start()

            def keep(i):
                own[p, zz, rows_of(i, CHUNK), :] = block[rows_of(here + i, CHUNK), :]

            each(0, t_col // CHUNK, keep)

        each(0, nz, step)
        if p == 0:
            load(1, "g").start()
            start_inputs(1)

    def forward_inputs(p):
        def step(k):
            source = lax.rem(z + nz - k, nz) * 2 + x
            inputs_copy(p, k, source, partner).wait_recv()
            inputs_forward(p, k, source).start()

        each(1, nz, step)

    def add_scaled(target, codes, scale, chunks):
        def step(i):
            at = rows_of(i, CHUNK)
            target[at, :] = target[at, :] + widen(codes[at, :], scale)

        each(0, chunks, step)

    def sum_x(p):
        chunks = t_col // CHUNK

        def step(k):
            zz = lax.rem(z + k, nz)
            xcopy(p, zz).wait_recv()
            add_scaled(own.at[p, zz], xrecv.at[p, zz], xrecv_s[p, zz, 0:1, 0:1], chunks)

            def store(i, value):
                xrecv[p, zz, rows_of(i, CHUNK), :] = value

            quantize(lambda i: own[p, zz, rows_of(i, CHUNK), :], store, put(xrecv_s, p, zz), chunks, width_g)
            zcopy(p, k, zz).start()

        each(1, nz, step)
        xcopy(p, z).wait_recv()
        add_scaled(own.at[p, z], xrecv.at[p, z], xrecv_s[p, z, 0:1, 0:1], chunks)

    def sum_z(p):
        chunks = t_col // CHUNK

        def step(k):
            zcopy(p, k, z).wait_recv()
            add_scaled(own.at[p, z], zrecv.at[p, k - 1], zrecv_s[p, k - 1, 0:1, 0:1], chunks)

        each(1, nz, step)

        def store(i, value):
            xrecv[p, z, rows_of(i, CHUNK), :] = value

        quantize(lambda i: own[p, z, rows_of(i, CHUNK), :], store, put(fin_s, p), chunks, width_g)
        scale_copy(p, 0, c, partner).start()
        each(1, nz, lambda k: scale_copy(p, k, c, zpeer(k)).start())

        def push(q):
            each(1, nz, lambda k: gather_copy(p, q, k, c, zpeer(k)).start())
            gather_copy(p, q, 0, c, partner).start()

        each(0, parts, push)
        pltpu.make_async_copy(xrecv.at[p, z], outs[p][0].at[c], local.at[p, 4]).start()
        pltpu.make_async_copy(fin_s.at[p], outs[p][1].at[c], local.at[p, 5]).start()

    def forward_scales(p):
        def step(k):
            source = lax.rem(z + nz - k, nz) * 2 + x
            scale_copy(p, k, source, partner).wait_recv()
            scale_forward(p, k, source).start()

        each(1, nz, step)

    def forward_gather(p, q):
        def step(k):
            source = lax.rem(z + nz - k, nz) * 2 + x
            gather_copy(p, q, k, source, partner).wait_recv()
            gather_forward(p, q, k, source).start()

        each(1, nz, step)

    def rotate_acts(p):
        load(p, "inputs").wait()
        load(p, "a").wait()
        inputs_copy(p, 0, z * 2 + 1 - x, partner).wait_recv()
        each(1, nz, lambda k: inputs_forward(p, k, lax.rem(z + nz - k, nz) * 2 + 1 - x).wait_recv())
        tile = min(512, width_a)
        chunks = t_row // CHUNK

        def rotate(piece):
            def columns(j):
                at = rows_of(j, tile)
                aown[p, :, at] = jnp.dot(
                    inputs_all[p, rows_of(piece, t_row), :], basis_a[0, :, at], preferred_element_type=F32
                )

            each(0, width_a // tile, columns)

        def step(k):
            piece = lax.rem(r + k, n_row)
            rotate(piece)

            def store(i, value):
                asend[p, k - 1, rows_of(i, CHUNK), :] = value

            quantize(lambda i: aown[p, rows_of(i, CHUNK), :], store, put(asend_s, p, k - 1), chunks, width_a)
            acopy(p, k, k - 1, r).start()

        each(1, n_row, step)
        rotate(r)
        if p == 0:
            load(1, "a").start()

    def sum_acts(p):
        chunks = t_row // CHUNK

        def step(k):
            source = lax.rem(r + n_row - k, n_row)
            acopy(p, k, k - 1, source).wait_recv()
            add_scaled(aown.at[p], arecv.at[p, source], arecv_s[p, source, 0:1, 0:1], chunks)

        each(1, n_row, step)

        def store(i, value):
            afin[p, rows_of(i, CHUNK), :] = value

        quantize(lambda i: aown[p, rows_of(i, CHUNK), :], store, put(afin_s, p), chunks, width_a)
        each(1, n_row, lambda k: act_gather(p, k, r).start())
        pltpu.make_async_copy(afin.at[p], outs[p][2].at[r], local.at[p, 6]).start()
        pltpu.make_async_copy(afin_s.at[p], outs[p][3].at[r], local.at[p, 7]).start()

    def own_copies(p):
        return [
            pltpu.make_async_copy(src, dst, local.at[p, 4 + at])
            for at, (src, dst) in enumerate(
                ((xrecv.at[p, z], outs[p][0].at[c]), (fin_s.at[p], outs[p][1].at[c]),
                 (afin.at[p], outs[p][2].at[r]), (afin_s.at[p], outs[p][3].at[r]))
            )
        ]

    blocks, per_block = tokens // depth, depth // t_col

    def prepare(p):
        for one in own_copies(p):
            one.wait()
        each(1, n_row, lambda k: act_gather(p, k, lax.rem(r + n_row - k, n_row)).wait_recv())
        both = (
            pltpu.make_async_copy(outs[p][2], arecv.at[p], codes_sem.at[0]),
            pltpu.make_async_copy(outs[p][3], arecv_s.at[p], codes_sem.at[1]),
        )
        for one in both:
            one.start()
        for one in both:
            one.wait()

        def split(piece):
            def step(i):
                value = widen(arecv[p, piece, rows_of(i, CHUNK), :], arecv_s[p, piece, 0:1, 0:1])
                high = value.astype(BF16)
                block_of, rows = place(piece * (t_row // CHUNK) + i, CHUNK)
                grads_all[0, block_of, rows, :] = high
                grads_all[1, block_of, rows, :] = (value - high.astype(F32)).astype(BF16)

            each(0, t_row // CHUNK, step)

        each(0, n_row, split)

    def arrived_scales(p):
        scale_copy(p, 0, z * 2 + 1 - x, partner).wait_recv()
        each(1, nz, lambda k: scale_forward(p, k, lax.rem(z + nz - k, nz) * 2 + 1 - x).wait_recv())
        copy = pltpu.make_async_copy(outs[p][1], codes_s, codes_sem.at[1])
        copy.start()
        copy.wait()

    def arrived(p, q):
        gather_copy(p, q, 0, z * 2 + 1 - x, partner).wait_recv()
        each(1, nz, lambda k: gather_forward(p, q, k, lax.rem(z + nz - k, nz) * 2 + 1 - x).wait_recv())

    def write(p, j):
        return pltpu.make_async_copy(stage, outs[p][4].at[rows_of(j, tile_g)], stage_sem.at[0])

    strip = min(512, width_a)
    strips = [pl.ds(n * strip, strip) for n in range(width_a // strip)]

    def multiply(m):
        b = marks[m]
        inside = masks[m, 0:1, :].astype(BF16)
        high, low = turned[b, :, pl.ds(0, depth)] * inside, turned[b, :, pl.ds(depth, depth)] * inside
        left = jnp.concatenate([high, high, low], axis=1)

        def part_of(at):
            a_high, a_low = grads_all[0, b, :, at], grads_all[1, b, :, at]
            right = jnp.concatenate([a_high, a_low, a_high], axis=0)
            return jnp.dot(left, right, preferred_element_type=F32)

        return part_of

    def product(p, j):
        copy = pltpu.make_async_copy(outs[p][0].at[:, :, rows_of(j, tile_g)], codes, codes_sem.at[0])
        copy.start()
        copy.wait()
        for b in range(blocks):
            at = pl.ds(b * per_block, per_block)
            value = widen(codes[at], codes_s[at, 0:1, 0:1]).reshape(depth, tile_g)
            high = value.astype(BF16)
            turned[b, :, pl.ds(0, depth)] = high.T
            turned[b, :, pl.ds(depth, depth)] = (value - high.astype(F32)).astype(BF16).T

        @pl.when(j >= 1)
        def _():
            write(p, j - 1).wait()

        part_of = multiply(0)
        for at in strips:
            total = part_of(at)
            acc[:, at] = total
            stage[:, at] = total * total * flags[1, 0]

        def step(m):
            part_of = multiply(m)
            for at in strips:
                total = acc[:, at] * flags[0, m] + part_of(at)
                acc[:, at] = total
                stage[:, at] = stage[:, at] + total * total * flags[1, m]

        each(1, marks.shape[0], step)
        write(p, j).start()

    tiles, per_part = width_g // tile_g, part // tile_g

    rotate_grads(0)
    forward_inputs(0)
    rotate_grads(1)
    sum_x(0)
    forward_inputs(1)
    rotate_acts(0)
    sum_z(0)
    sum_x(1)
    sum_acts(0)
    forward_scales(0)
    prepare(0)
    rotate_acts(1)
    each(0, parts, lambda q: forward_gather(0, q))
    sum_z(1)
    sum_acts(1)
    forward_scales(1)
    arrived_scales(0)

    def overlap(q):
        arrived(0, q)
        each(q * per_part, (q + 1) * per_part, lambda j: product(0, j))
        forward_gather(1, q)

    def last(q):
        arrived(1, q)
        each(q * per_part, (q + 1) * per_part, lambda j: product(1, j))

    def drain(p):
        write(p, tiles - 1).wait()

    each(0, parts, overlap)
    drain(0)
    prepare(1)
    arrived_scales(1)
    each(0, parts, last)
    drain(1)

    for p in (0, 1):

        def departures(k):
            source = lax.rem(z + nz - k, nz) * 2 + x
            scale_forward(p, k, source).wait_send()
            scale_copy(p, k, c, zpeer(k)).wait_send()
            each(0, parts, lambda q: gather_forward(p, q, k, source).wait_send())
            each(0, parts, lambda q: gather_copy(p, q, k, c, zpeer(k)).wait_send())
            inputs_copy(p, k, c, zpeer(k)).wait_send()
            inputs_forward(p, k, source).wait_send()
            zcopy(p, k, lax.rem(z + k, nz)).wait_send()

        each(1, nz, departures)

        def row_departures(k):
            act_gather(p, k, r).wait_send()
            acopy(p, k, k - 1, r).wait_send()
            grads_copy(p, k, r).wait_send()

        each(1, n_row, row_departures)
        each(0, nz, lambda zz: xcopy(p, zz).wait_send())
        inputs_copy(p, 0, c, partner).wait_send()
        scale_copy(p, 0, c, partner).wait_send()
        each(0, parts, lambda q: gather_copy(p, q, 0, c, partner).wait_send())


def segments(seq_ids, tokens, depth):
    starts = jnp.sum((seq_ids[None, :] < jnp.arange(1, SEQS, dtype=I32)[:, None]).astype(I32), axis=1)
    cuts = jnp.sort(jnp.concatenate([starts, jnp.arange(depth, tokens, depth, dtype=I32)]))
    low = jnp.concatenate([jnp.zeros((1,), I32), cuts])
    high = jnp.concatenate([cuts, jnp.full((1,), tokens, I32)])
    block = jnp.minimum(low // depth, tokens // depth - 1)
    numbers = jnp.sum((starts[None, :] <= low[:, None]).astype(I32), axis=1)
    same = (numbers[1:] == numbers[:-1]).astype(F32)
    goes_on = jnp.concatenate([jnp.zeros((1,), F32), same])
    ends = jnp.concatenate([1.0 - same, jnp.ones((1,), F32)]) / SEQS
    tokens_of = block[:, None] * depth + jnp.arange(depth, dtype=I32)[None, :]
    inside = ((tokens_of >= low[:, None]) & (tokens_of < high[:, None])).astype(F32)
    return block, jnp.stack([goes_on, ends]), jnp.repeat(inside[:, None, :], 8, axis=1)


def rotate(n_row, n_col, seq_ids, query, output):
    inputs, grads, act_basis, grad_basis = query
    t_col, feats_a = inputs.shape
    t_row, feats_g = grads.shape
    width_a, width_g = act_basis.shape[1], grad_basis.shape[1]
    tokens, nz = t_col * n_col, n_col // 2
    one = (
        jax.ShapeDtypeStruct((n_col, t_col, width_g), I16),
        jax.ShapeDtypeStruct((n_col, 8, 128), F32),
        jax.ShapeDtypeStruct((n_row, t_row, width_a), I16),
        jax.ShapeDtypeStruct((n_row, 8, 128), F32),
        jax.ShapeDtypeStruct((width_g, width_a), F32),
    )
    depth, tile_g = min(256, tokens), min(512, width_g)
    parts = max(1, min(4, width_g // tile_g))
    marks, flags, masks = segments(seq_ids, tokens, depth)
    dma = pltpu.SemaphoreType.DMA
    flops = 4 * tokens * (feats_a * width_a + feats_g * width_g + 6 * width_g * width_a)
    results = pl.pallas_call(
        functools.partial(rotate_kernel, n_row, n_col, depth, tile_g, parts),
        out_shape=one + one,
        in_specs=[pl.BlockSpec(memory_space=pltpu.SMEM)] * 2
        + [pl.BlockSpec(memory_space=pltpu.VMEM)]
        + [pl.BlockSpec(memory_space=pl.ANY)] * 8,
        out_specs=[pl.BlockSpec(memory_space=pl.ANY)] * 10,
        scratch_shapes=[
            pltpu.VMEM((2, tokens // depth, depth, feats_g), BF16),
            pltpu.VMEM((2, tokens, feats_a), BF16),
            pltpu.VMEM((1, feats_g, width_g), BF16),
            pltpu.VMEM((1, feats_a, width_a), BF16),
            pltpu.VMEM((2 * t_col, width_g), F32),
            pltpu.VMEM((2, nz, t_col, width_g), F32),
            pltpu.VMEM((2, nz, t_col, width_g), I16),
            pltpu.VMEM((2, nz, 8, 128), F32),
            pltpu.VMEM((2, nz, t_col, width_g), I16),
            pltpu.VMEM((2, nz, 8, 128), F32),
            pltpu.VMEM((2, nz - 1, t_col, width_g), I16),
            pltpu.VMEM((2, nz - 1, 8, 128), F32),
            pltpu.VMEM((2, 8, 128), F32),
            pltpu.VMEM((2, t_row, width_a), F32),
            pltpu.VMEM((2, n_row - 1, t_row, width_a), I16),
            pltpu.VMEM((2, n_row - 1, 8, 128), F32),
            pltpu.VMEM((2, n_row, t_row, width_a), I16),
            pltpu.VMEM((2, n_row, 8, 128), F32),
            pltpu.VMEM((2, t_row, width_a), I16),
            pltpu.VMEM((2, 8, 128), F32),
            pltpu.VMEM((n_col, t_col, tile_g), I16),
            pltpu.VMEM((n_col, 8, 128), F32),
            pltpu.VMEM((tokens // depth, tile_g, 2 * depth), BF16),
            pltpu.VMEM((tile_g, width_a), F32),
            pltpu.VMEM((tile_g, width_a), F32),
            dma((2, n_row)), dma((2, n_row)),
            dma((2, nz)), dma((2, nz)), dma((2, n_col)),
            dma((2, nz, 2)), dma((2, nz, 2)), dma((2, nz, 2)), dma((2, nz, 2)),
            dma((2, nz, parts + 1)), dma((2, nz, parts + 1)), dma((2, n_col, parts + 1)),
            dma((2, n_row, 2)), dma((2, n_row, 2)), dma((2, n_row, 2)), dma((2, n_row, 2)),
            dma((2, 8)), dma((2,)), dma((1,)),
        ],
        compiler_params=pltpu.CompilerParams(
            collective_id=0, has_side_effects=True, vmem_limit_bytes=62 * 2**20
        ),
        cost_estimate=pl.CostEstimate(flops=flops, bytes_accessed=32 * 2**20, transcendentals=0),
        name="rotate",
    )(marks, flags, masks, *query, *output)
    return results[4], results[9]


def per_device(n_row, n_col, seq_ids, *args):
    return rotate(n_row, n_col, seq_ids, args[:4], args[4:])


def solution(mesh):
    one = (P("col", "row"), P("row", "col"), P("row", "col"), P("col", "row"))
    return jax.shard_map(
        functools.partial(per_device, mesh.shape["row"], mesh.shape["col"]),
        mesh=mesh,
        in_specs=(P(),) + one + one,
        out_specs=(P("row", "col"), P("row", "col")),
        check_vma=False,
    )
```

```python
import functools

import jax
import jax.numpy as jnp
from jax import lax
from jax.experimental import pallas as pl
from jax.experimental.pallas import tpu as pltpu
from jax.sharding import PartitionSpec as P

SEQS = 4
CHUNK = 16
TOP = 32767.0
MESH = pl.DeviceIdType.MESH
F32, BF16, I16, I32 = jnp.float32, jnp.bfloat16, jnp.int16, jnp.int32


def quantize(load, store, store_scale, chunks, width):
    most = lax.fori_loop(
        0, chunks, lambda i, m: jnp.maximum(m, jnp.abs(load(i))), jnp.zeros((CHUNK, width), F32)
    )
    most = jnp.max(jnp.max(most, axis=1, keepdims=True), axis=0, keepdims=True)
    inverse = jnp.where(most > 1e-30, TOP / jnp.maximum(most, 1e-30), 0.0)
    store_scale(jnp.broadcast_to(most * (1.0 / TOP), (8, 128)))

    def body(i, carry):
        store(i, jnp.round(load(i) * inverse).astype(I32).astype(I16))
        return carry

    lax.fori_loop(0, chunks, body, 0)


def widen(codes, scale):
    return codes.astype(I32).astype(F32) * scale


def rows_of(i, size):
    return pl.ds(pl.multiple_of(i * size, size), size)


def rotate_kernel(n_row, n_col, depth, tile_g, parts, marks, flags, masks, *refs):
    ins, refs = (refs[0:4], refs[4:8]), refs[8:]
    outs, refs = (refs[0:5], refs[5:10]), refs[10:]
    (grads_all, inputs_all, basis_g, basis_a, block, own, xsend, xsend_s, xrecv, xrecv_s, zrecv, zrecv_s,
     fin_s, aown, asend, asend_s, arecv, arecv_s, afin, afin_s,
     codes, codes_s, turned, acc, stage,
     g_send, g_recv, i_send, f_send, i_recv, xs_send, xs_recv, zs_send, zs_recv,
     ag_send, agf_send, ag_recv, as_send, as_recv, aa_send, aa_recv, local, codes_sem, stage_sem) = refs

    r, c = lax.axis_index("row"), lax.axis_index("col")
    nz = n_col // 2
    z, x = c // 2, lax.rem(c, 2)
    partner = (r, z * 2 + 1 - x)
    tokens = grads_all.shape[1] * grads_all.shape[2]
    feats_a = basis_a.shape[1]
    width_g, width_a = basis_g.shape[2], basis_a.shape[2]
    t_col, t_row = tokens // n_col, tokens // n_row

    def zpeer(k):
        return (r, lax.rem(z + k, nz) * 2 + x)

    def rpeer(k):
        return (lax.rem(r + k, n_row), c)

    def rdma(src, dst, send, recv, device):
        return pltpu.make_async_remote_copy(
            src_ref=src, dst_ref=dst, send_sem=send, recv_sem=recv, device_id=device, device_id_type=MESH
        )

    class pair:
        def __init__(self, src, src_s, dst, dst_s, send, recv, device):
            self.both = (
                rdma(src, dst, send.at[0], recv.at[0], device),
                rdma(src_s, dst_s, send.at[1], recv.at[1], device),
            )

        def start(self):
            for one in self.both:
                one.start()

        def wait_send(self):
            for one in self.both:
                one.wait_send()

        def wait_recv(self):
            for one in self.both:
                one.wait_recv()

    def each(low, high, body):
        lax.fori_loop(low, high, lambda i, carry: (body(i), carry)[1], 0)

    barrier = pltpu.get_barrier_semaphore()

    def greet(device):
        pl.semaphore_signal(barrier, inc=1, device_id=device, device_id_type=MESH)

    greet(partner)
    each(1, nz, lambda k: greet(zpeer(k)))
    each(1, n_row, lambda k: greet(rpeer(k)))
    pl.semaphore_wait(barrier, 1 + (nz - 1) + (n_row - 1))

    def place(i, size):
        runs = depth // size
        return lax.div(i, runs), rows_of(lax.rem(i, runs), size)

    def load(p, kind):
        if kind == "g":
            return pltpu.make_async_copy(ins[p][3], basis_g.at[0], local.at[p, 0])
        if kind == "a":
            return pltpu.make_async_copy(ins[p][2], basis_a.at[0], local.at[p, 1])
        if kind == "inputs":
            return pltpu.make_async_copy(ins[p][0], inputs_all.at[p, rows_of(c, t_col)], local.at[p, 2])
        return pltpu.make_async_copy(ins[p][1], grads_all.at[p, *place(r, t_row)], local.at[p, 3])

    def grads_copy(p, k, source):
        return rdma(ins[p][1], grads_all.at[p, *place(source, t_row)], g_send.at[p, k], g_recv.at[p, source], rpeer(k))

    def inputs_copy(p, k, source, device):
        return rdma(ins[p][0], inputs_all.at[p, rows_of(source, t_col)], i_send.at[p, k], i_recv.at[p, source], device)

    def inputs_forward(p, k, source):
        there = inputs_all.at[p, rows_of(source, t_col)]
        return rdma(there, there, f_send.at[p, k], i_recv.at[p, source], partner)

    def start_grads(p):
        load(p, "grads").start()
        each(1, n_row, lambda k: grads_copy(p, k, r).start())

    def start_inputs(p):
        load(p, "inputs").start()
        each(1, nz, lambda k: inputs_copy(p, k, c, zpeer(k)).start())

    start_grads(0)
    start_inputs(0)
    inputs_copy(0, 0, c, partner).start()
    inputs_copy(1, 0, c, partner).start()
    load(0, "g").start()
    load(0, "a").start()

    def xcopy(p, zz):
        return pair(xsend.at[p, zz], xsend_s.at[p, zz], xrecv.at[p, zz], xrecv_s.at[p, zz],
                    xs_send.at[p, zz], xs_recv.at[p, zz], partner)

    def zcopy(p, k, slot):
        return pair(xrecv.at[p, slot], xrecv_s.at[p, slot], zrecv.at[p, k - 1], zrecv_s.at[p, k - 1],
                    zs_send.at[p, k], zs_recv.at[p, k], zpeer(k))

    part = width_g // parts

    def columns_of(q):
        return pl.ds(pl.multiple_of(q * part, part), part)

    def gather_copy(p, q, k, source, device):
        return rdma(xrecv.at[p, z, :, columns_of(q)], outs[p][0].at[source, :, columns_of(q)],
                    ag_send.at[p, k, q], ag_recv.at[p, source, q], device)

    def gather_forward(p, q, k, source):
        there = outs[p][0].at[source, :, columns_of(q)]
        return rdma(there, there, agf_send.at[p, k, q], ag_recv.at[p, source, q], partner)

    def scale_copy(p, k, source, device):
        return rdma(fin_s.at[p], outs[p][1].at[source], ag_send.at[p, k, parts], ag_recv.at[p, source, parts], device)

    def scale_forward(p, k, source):
        there = outs[p][1].at[source]
        return rdma(there, there, agf_send.at[p, k, parts], ag_recv.at[p, source, parts], partner)

    def acopy(p, k, slot, source):
        return pair(asend.at[p, slot], asend_s.at[p, slot], arecv.at[p, source], arecv_s.at[p, source],
                    as_send.at[p, k], as_recv.at[p, source], rpeer(k))

    def act_gather(p, k, source):
        return pair(afin.at[p], afin_s.at[p], outs[p][2].at[source], outs[p][3].at[source],
                    aa_send.at[p, k], aa_recv.at[p, source], rpeer(k))

    def put(ref, *at):
        def store(value):
            ref[at] = value

        return store

    def rotate_grads(p):
        load(p, "grads").wait()
        load(p, "g").wait()
        each(1, n_row, lambda k: grads_copy(p, k, lax.rem(r + n_row - k, n_row)).wait_recv())
        if p == 0:
            start_grads(1)
        tile = min(512, width_g)

        def step(k):
            zz = lax.rem(z + k, nz)

            def columns(j):
                at = rows_of(j, tile)
                block[:, at] = jnp.dot(
                    grads_all[p, *place(zz, 2 * t_col), :], basis_g[0, :, at], preferred_element_type=F32
                )

            each(0, width_g // tile, columns)
            there, here = (1 - x) * (t_col // CHUNK), x * (t_col // CHUNK)

            def store(i, value):
                xsend[p, zz, rows_of(i, CHUNK), :] = value

            quantize(lambda i: block[rows_of(there + i, CHUNK), :], store, put(xsend_s, p, zz),
                     t_col // CHUNK, width_g)
            xcopy(p, zz).start()

            def keep(i):
                own[p, zz, rows_of(i, CHUNK), :] = block[rows_of(here + i, CHUNK), :]

            each(0, t_col // CHUNK, keep)

        each(0, nz, step)
        if p == 0:
            load(1, "g").start()
            start_inputs(1)

    def forward_inputs(p):
        def step(k):
            source = lax.rem(z + nz - k, nz) * 2 + x
            inputs_copy(p, k, source, partner).wait_recv()
            inputs_forward(p, k, source).start()

        each(1, nz, step)

    def add_scaled(target, codes, scale, chunks):
        def step(i):
            at = rows_of(i, CHUNK)
            target[at, :] = target[at, :] + widen(codes[at, :], scale)

        each(0, chunks, step)

    def sum_x(p):
        chunks = t_col // CHUNK

        def step(k):
            zz = lax.rem(z + k, nz)
            xcopy(p, zz).wait_recv()
            add_scaled(own.at[p, zz], xrecv.at[p, zz], xrecv_s[p, zz, 0:1, 0:1], chunks)

            def store(i, value):
                xrecv[p, zz, rows_of(i, CHUNK), :] = value

            quantize(lambda i: own[p, zz, rows_of(i, CHUNK), :], store, put(xrecv_s, p, zz), chunks, width_g)
            zcopy(p, k, zz).start()

        each(1, nz, step)
        xcopy(p, z).wait_recv()
        add_scaled(own.at[p, z], xrecv.at[p, z], xrecv_s[p, z, 0:1, 0:1], chunks)

    def sum_z(p):
        chunks = t_col // CHUNK

        def step(k):
            zcopy(p, k, z).wait_recv()
            add_scaled(own.at[p, z], zrecv.at[p, k - 1], zrecv_s[p, k - 1, 0:1, 0:1], chunks)

        each(1, nz, step)

        def store(i, value):
            xrecv[p, z, rows_of(i, CHUNK), :] = value

        quantize(lambda i: own[p, z, rows_of(i, CHUNK), :], store, put(fin_s, p), chunks, width_g)
        scale_copy(p, 0, c, partner).start()
        each(1, nz, lambda k: scale_copy(p, k, c, zpeer(k)).start())

        def push(q):
            each(1, nz, lambda k: gather_copy(p, q, k, c, zpeer(k)).start())
            gather_copy(p, q, 0, c, partner).start()

        each(0, parts, push)
        pltpu.make_async_copy(xrecv.at[p, z], outs[p][0].at[c], local.at[p, 4]).start()
        pltpu.make_async_copy(fin_s.at[p], outs[p][1].at[c], local.at[p, 5]).start()

    def forward_scales(p):
        def step(k):
            source = lax.rem(z + nz - k, nz) * 2 + x
            scale_copy(p, k, source, partner).wait_recv()
            scale_forward(p, k, source).start()

        each(1, nz, step)

    def forward_gather(p, q):
        def step(k):
            source = lax.rem(z + nz - k, nz) * 2 + x
            gather_copy(p, q, k, source, partner).wait_recv()
            gather_forward(p, q, k, source).start()

        each(1, nz, step)

    def rotate_acts(p):
        load(p, "inputs").wait()
        load(p, "a").wait()
        inputs_copy(p, 0, z * 2 + 1 - x, partner).wait_recv()
        each(1, nz, lambda k: inputs_forward(p, k, lax.rem(z + nz - k, nz) * 2 + 1 - x).wait_recv())
        tile = min(512, width_a)
        chunks = t_row // CHUNK

        def rotate(piece):
            def columns(j):
                at = rows_of(j, tile)
                aown[p, :, at] = jnp.dot(
                    inputs_all[p, rows_of(piece, t_row), :], basis_a[0, :, at], preferred_element_type=F32
                )

            each(0, width_a // tile, columns)

        def step(k):
            piece = lax.rem(r + k, n_row)
            rotate(piece)

            def store(i, value):
                asend[p, k - 1, rows_of(i, CHUNK), :] = value

            quantize(lambda i: aown[p, rows_of(i, CHUNK), :], store, put(asend_s, p, k - 1), chunks, width_a)
            acopy(p, k, k - 1, r).start()

        each(1, n_row, step)
        rotate(r)
        if p == 0:
            load(1, "a").start()

    def sum_acts(p):
        chunks = t_row // CHUNK

        def step(k):
            source = lax.rem(r + n_row - k, n_row)
            acopy(p, k, k - 1, source).wait_recv()
            add_scaled(aown.at[p], arecv.at[p, source], arecv_s[p, source, 0:1, 0:1], chunks)

        each(1, n_row, step)

        def store(i, value):
            afin[p, rows_of(i, CHUNK), :] = value

        quantize(lambda i: aown[p, rows_of(i, CHUNK), :], store, put(afin_s, p), chunks, width_a)
        each(1, n_row, lambda k: act_gather(p, k, r).start())
        pltpu.make_async_copy(afin.at[p], outs[p][2].at[r], local.at[p, 6]).start()
        pltpu.make_async_copy(afin_s.at[p], outs[p][3].at[r], local.at[p, 7]).start()

    def own_copies(p):
        return [
            pltpu.make_async_copy(src, dst, local.at[p, 4 + at])
            for at, (src, dst) in enumerate(
                ((xrecv.at[p, z], outs[p][0].at[c]), (fin_s.at[p], outs[p][1].at[c]),
                 (afin.at[p], outs[p][2].at[r]), (afin_s.at[p], outs[p][3].at[r]))
            )
        ]

    blocks, per_block = tokens // depth, depth // t_col

    def prepare(p):
        for one in own_copies(p):
            one.wait()
        each(1, n_row, lambda k: act_gather(p, k, lax.rem(r + n_row - k, n_row)).wait_recv())
        both = (
            pltpu.make_async_copy(outs[p][2], arecv.at[p], codes_sem.at[0]),
            pltpu.make_async_copy(outs[p][3], arecv_s.at[p], codes_sem.at[1]),
        )
        for one in both:
            one.start()
        for one in both:
            one.wait()

        def split(piece):
            def step(i):
                value = widen(arecv[p, piece, rows_of(i, CHUNK), :], arecv_s[p, piece, 0:1, 0:1])
                high = value.astype(BF16)
                block_of, rows = place(piece * (t_row // CHUNK) + i, CHUNK)
                grads_all[0, block_of, rows, :] = high
                grads_all[1, block_of, rows, :] = (value - high.astype(F32)).astype(BF16)

            each(0, t_row // CHUNK, step)

        each(0, n_row, split)

    def arrived_scales(p):
        scale_copy(p, 0, z * 2 + 1 - x, partner).wait_recv()
        each(1, nz, lambda k: scale_forward(p, k, lax.rem(z + nz - k, nz) * 2 + 1 - x).wait_recv())
        copy = pltpu.make_async_copy(outs[p][1], codes_s, codes_sem.at[1])
        copy.start()
        copy.wait()

    def arrived(p, q):
        gather_copy(p, q, 0, z * 2 + 1 - x, partner).wait_recv()
        each(1, nz, lambda k: gather_forward(p, q, k, lax.rem(z + nz - k, nz) * 2 + 1 - x).wait_recv())

    def write(p, j):
        return pltpu.make_async_copy(stage, outs[p][4].at[rows_of(j, tile_g)], stage_sem.at[0])

    strip = min(512, width_a)
    strips = [pl.ds(n * strip, strip) for n in range(width_a // strip)]

    def multiply(m):
        b = marks[m]
        inside = masks[m, 0:1, :].astype(BF16)
        high, low = turned[b, :, pl.ds(0, depth)] * inside, turned[b, :, pl.ds(depth, depth)] * inside
        left = jnp.concatenate([high, high, low], axis=1)

        def part_of(at):
            a_high, a_low = grads_all[0, b, :, at], grads_all[1, b, :, at]
            right = jnp.concatenate([a_high, a_low, a_high], axis=0)
            return jnp.dot(left, right, preferred_element_type=F32)

        return part_of

    def product(p, j):
        copy = pltpu.make_async_copy(outs[p][0].at[:, :, rows_of(j, tile_g)], codes, codes_sem.at[0])
        copy.start()
        copy.wait()
        for b in range(blocks):
            at = pl.ds(b * per_block, per_block)
            value = widen(codes[at], codes_s[at, 0:1, 0:1]).reshape(depth, tile_g)
            high = value.astype(BF16)
            turned[b, :, pl.ds(0, depth)] = high.T
            turned[b, :, pl.ds(depth, depth)] = (value - high.astype(F32)).astype(BF16).T

        @pl.when(j >= 1)
        def _():
            write(p, j - 1).wait()

        part_of = multiply(0)
        for at in strips:
            total = part_of(at)
            acc[:, at] = total
            stage[:, at] = total * total * flags[1, 0]

        def step(m):
            part_of = multiply(m)
            for at in strips:
                total = acc[:, at] * flags[0, m] + part_of(at)
                acc[:, at] = total
                stage[:, at] = stage[:, at] + total * total * flags[1, m]

        each(1, marks.shape[0], step)
        write(p, j).start()

    tiles, per_part = width_g // tile_g, part // tile_g

    rotate_grads(0)
    forward_inputs(0)
    rotate_grads(1)
    sum_x(0)
    forward_inputs(1)
    rotate_acts(0)
    sum_z(0)
    sum_x(1)
    sum_acts(0)
    forward_scales(0)
    each(0, parts, lambda q: forward_gather(0, q))
    rotate_acts(1)
    sum_z(1)
    sum_acts(1)
    prepare(0)
    forward_scales(1)
    arrived_scales(0)

    def overlap(q):
        arrived(0, q)
        each(q * per_part, (q + 1) * per_part, lambda j: product(0, j))
        forward_gather(1, q)

    def last(q):
        arrived(1, q)
        each(q * per_part, (q + 1) * per_part, lambda j: product(1, j))

    def drain(p):
        write(p, tiles - 1).wait()

    each(0, parts, overlap)
    drain(0)
    prepare(1)
    arrived_scales(1)
    each(0, parts, last)
    drain(1)

    for p in (0, 1):

        def departures(k):
            source = lax.rem(z + nz - k, nz) * 2 + x
            scale_forward(p, k, source).wait_send()
            scale_copy(p, k, c, zpeer(k)).wait_send()
            each(0, parts, lambda q: gather_forward(p, q, k, source).wait_send())
            each(0, parts, lambda q: gather_copy(p, q, k, c, zpeer(k)).wait_send())
            inputs_copy(p, k, c, zpeer(k)).wait_send()
            inputs_forward(p, k, source).wait_send()
            zcopy(p, k, lax.rem(z + k, nz)).wait_send()

        each(1, nz, departures)

        def row_departures(k):
            act_gather(p, k, r).wait_send()
            acopy(p, k, k - 1, r).wait_send()
            grads_copy(p, k, r).wait_send()

        each(1, n_row, row_departures)
        each(0, nz, lambda zz: xcopy(p, zz).wait_send())
        inputs_copy(p, 0, c, partner).wait_send()
        scale_copy(p, 0, c, partner).wait_send()
        each(0, parts, lambda q: gather_copy(p, q, 0, c, partner).wait_send())


def segments(seq_ids, tokens, depth):
    starts = jnp.sum((seq_ids[None, :] < jnp.arange(1, SEQS, dtype=I32)[:, None]).astype(I32), axis=1)
    cuts = jnp.sort(jnp.concatenate([starts, jnp.arange(depth, tokens, depth, dtype=I32)]))
    low = jnp.concatenate([jnp.zeros((1,), I32), cuts])
    high = jnp.concatenate([cuts, jnp.full((1,), tokens, I32)])
    block = jnp.minimum(low // depth, tokens // depth - 1)
    numbers = jnp.sum((starts[None, :] <= low[:, None]).astype(I32), axis=1)
    same = (numbers[1:] == numbers[:-1]).astype(F32)
    goes_on = jnp.concatenate([jnp.zeros((1,), F32), same])
    ends = jnp.concatenate([1.0 - same, jnp.ones((1,), F32)]) / SEQS
    tokens_of = block[:, None] * depth + jnp.arange(depth, dtype=I32)[None, :]
    inside = ((tokens_of >= low[:, None]) & (tokens_of < high[:, None])).astype(F32)
    return block, jnp.stack([goes_on, ends]), jnp.repeat(inside[:, None, :], 8, axis=1)


def rotate(n_row, n_col, seq_ids, query, output):
    inputs, grads, act_basis, grad_basis = query
    t_col, feats_a = inputs.shape
    t_row, feats_g = grads.shape
    width_a, width_g = act_basis.shape[1], grad_basis.shape[1]
    tokens, nz = t_col * n_col, n_col // 2
    one = (
        jax.ShapeDtypeStruct((n_col, t_col, width_g), I16),
        jax.ShapeDtypeStruct((n_col, 8, 128), F32),
        jax.ShapeDtypeStruct((n_row, t_row, width_a), I16),
        jax.ShapeDtypeStruct((n_row, 8, 128), F32),
        jax.ShapeDtypeStruct((width_g, width_a), F32),
    )
    depth, tile_g = min(256, tokens), min(512, width_g)
    parts = max(1, min(4, width_g // tile_g))
    marks, flags, masks = segments(seq_ids, tokens, depth)
    dma = pltpu.SemaphoreType.DMA
    flops = 4 * tokens * (feats_a * width_a + feats_g * width_g + 6 * width_g * width_a)
    results = pl.pallas_call(
        functools.partial(rotate_kernel, n_row, n_col, depth, tile_g, parts),
        out_shape=one + one,
        in_specs=[pl.BlockSpec(memory_space=pltpu.SMEM)] * 2
        + [pl.BlockSpec(memory_space=pltpu.VMEM)]
        + [pl.BlockSpec(memory_space=pl.ANY)] * 8,
        out_specs=[pl.BlockSpec(memory_space=pl.ANY)] * 10,
        scratch_shapes=[
            pltpu.VMEM((2, tokens // depth, depth, feats_g), BF16),
            pltpu.VMEM((2, tokens, feats_a), BF16),
            pltpu.VMEM((1, feats_g, width_g), BF16),
            pltpu.VMEM((1, feats_a, width_a), BF16),
            pltpu.VMEM((2 * t_col, width_g), F32),
            pltpu.VMEM((2, nz, t_col, width_g), F32),
            pltpu.VMEM((2, nz, t_col, width_g), I16),
            pltpu.VMEM((2, nz, 8, 128), F32),
            pltpu.VMEM((2, nz, t_col, width_g), I16),
            pltpu.VMEM((2, nz, 8, 128), F32),
            pltpu.VMEM((2, nz - 1, t_col, width_g), I16),
            pltpu.VMEM((2, nz - 1, 8, 128), F32),
            pltpu.VMEM((2, 8, 128), F32),
            pltpu.VMEM((2, t_row, width_a), F32),
            pltpu.VMEM((2, n_row - 1, t_row, width_a), I16),
            pltpu.VMEM((2, n_row - 1, 8, 128), F32),
            pltpu.VMEM((2, n_row, t_row, width_a), I16),
            pltpu.VMEM((2, n_row, 8, 128), F32),
            pltpu.VMEM((2, t_row, width_a), I16),
            pltpu.VMEM((2, 8, 128), F32),
            pltpu.VMEM((n_col, t_col, tile_g), I16),
            pltpu.VMEM((n_col, 8, 128), F32),
            pltpu.VMEM((tokens // depth, tile_g, 2 * depth), BF16),
            pltpu.VMEM((tile_g, width_a), F32),
            pltpu.VMEM((tile_g, width_a), F32),
            dma((2, n_row)), dma((2, n_row)),
            dma((2, nz)), dma((2, nz)), dma((2, n_col)),
            dma((2, nz, 2)), dma((2, nz, 2)), dma((2, nz, 2)), dma((2, nz, 2)),
            dma((2, nz, parts + 1)), dma((2, nz, parts + 1)), dma((2, n_col, parts + 1)),
            dma((2, n_row, 2)), dma((2, n_row, 2)), dma((2, n_row, 2)), dma((2, n_row, 2)),
            dma((2, 8)), dma((2,)), dma((1,)),
        ],
        compiler_params=pltpu.CompilerParams(
            collective_id=0, has_side_effects=True, vmem_limit_bytes=62 * 2**20
        ),
        cost_estimate=pl.CostEstimate(flops=flops, bytes_accessed=32 * 2**20, transcendentals=0),
        name="rotate",
    )(marks, flags, masks, *query, *output)
    return results[4], results[9]


def per_device(n_row, n_col, seq_ids, *args):
    return rotate(n_row, n_col, seq_ids, args[:4], args[4:])


def solution(mesh):
    one = (P("col", "row"), P("row", "col"), P("row", "col"), P("col", "row"))
    return jax.shard_map(
        functools.partial(per_device, mesh.shape["row"], mesh.shape["col"]),
        mesh=mesh,
        in_specs=(P(),) + one + one,
        out_specs=(P("row", "col"), P("row", "col")),
        check_vma=False,
    )
```
